32 devices in a mesh: node: 8 (over z, x), feat: 4 (over y, core).
Axes of the slice: x: 2, y: 2, z: 4, core: 2. Of those that a mesh axis runs over, the one named last changes fastest.
Arguments:
- features: float32 [6144, 1024], P('node', 'feat'), may hold values from -6 to 6
- degrees: int32 [6144], P('node'), may hold values from 1 to 4
- tile_row: int32 [8, 33], P('node'), may hold values from 0 to 5, as said below
- tile_col: int32 [8, 33], P('node'), may hold values from 0 to 13, as said below
- tile_count: int32 [8], P('node'), may hold values from 19 to 33, as said below
- send_block: int32 [8, 8], replicated, may hold values from 0 to 5
- tile_val: bfloat16 [8, 33, 128, 128], P('node'), may hold values from -0.15625 to 0.15625
- weight: bfloat16 [1024, 3, 1024], P('node', None, 'feat'), may hold values from -0.109375 to 0.109375
- out_bias: float32 [1024], replicated, may hold values from -3 to 3
- cotangent: bfloat16 [6144, 1024], P(('node', 'feat')), may hold values from -0.076171875 to 0.076171875
Outputs:
- output: bfloat16 [6144, 1024], P(('node', 'feat'))
- weight_grad: float32 [1024, 3, 1024], P('node', None, 'feat')
- bias_grad: float32 [1024], replicated
The draws below stay inside these ranges and needn't reach their ends.
Inputs may be any that keep to these rules, and one draw needn't show every extreme that they name: `tile_row`: the row block of each slot; for each other part q, between 1 and 3 live tiles of part p read slot 6 + q, each at a different row block. `tile_col`: below 6: the part's own row block; 6 + q: the block that part q sends; the first 12 slots of each part read own blocks, tile i < 6 at row block i, column i; slots past tile_count read 0; no tile reads slot 6 + p in part p. `tile_count`: live tiles come first in each part; some part has 33 live tiles.
All inputs are finite; a program needn't handle non-finite values.
Results may differ from the reference program's by a relative error of at most 0.0057.
Values may be sent and summed in bfloat16 or wider, within the bound.
A program may use at most 192 MiB of HBM per device.

```python
import jax
import jax.numpy as jnp
from jax import lax

F = 1024
OUT = 1024
HOPS = 2
BLOCK = 128
RB = 6
MULT = 3
PARTS_SIZE = 8
NBLOCKS = 48
NODES = 6144
TILES_DEV = 33


def graph_tables(key):
    key = jax.random.fold_in(key, 4242)
    keys = jax.random.split(key, 5)
    send_block = jax.random.randint(keys[0], (PARTS_SIZE, PARTS_SIZE), 0, RB)
    busiest = jax.random.randint(keys[1], (), 0, PARTS_SIZE)
    level = jax.random.randint(keys[2], (PARTS_SIZE, PARTS_SIZE), 0, 10)
    multiple = jnp.where(level < 8, 1, jnp.where(level < 9, 2, MULT))
    part_ids = jnp.arange(PARTS_SIZE, dtype=jnp.int32)
    multiple = jnp.where(part_ids[:, None] == busiest, MULT, multiple)
    multiple = jnp.where(part_ids[:, None] == part_ids[None, :], 0, multiple)
    order_keys = jax.random.randint(keys[3], (PARTS_SIZE, PARTS_SIZE, RB), 0, 1 << 20) * RB + jnp.arange(RB, dtype=jnp.int32)
    row_choice = jnp.argsort(order_keys, axis=-1)[:, :, :MULT].astype(jnp.int32)
    slot_ids = jnp.arange(MULT, dtype=jnp.int32)
    valid = slot_ids[None, None, :] < multiple[:, :, None]
    flat_valid = valid.reshape(PARTS_SIZE, PARTS_SIZE * MULT)
    flat_rows = row_choice.reshape(PARTS_SIZE, PARTS_SIZE * MULT)
    flat_source = jnp.broadcast_to(part_ids[None, :, None], (PARTS_SIZE, PARTS_SIZE, MULT)).reshape(PARTS_SIZE, PARTS_SIZE * MULT)
    rank = jnp.where(flat_valid, 0, 1) * (PARTS_SIZE * MULT) + jnp.arange(PARTS_SIZE * MULT, dtype=jnp.int32)
    picked = jnp.argsort(rank, axis=-1)[:, :MULT * (PARTS_SIZE - 1)]
    remote_valid = jnp.take_along_axis(flat_valid, picked, axis=1)
    remote_row = jnp.where(remote_valid, jnp.take_along_axis(flat_rows, picked, axis=1), 0)
    remote_col = jnp.where(remote_valid, RB + jnp.take_along_axis(flat_source, picked, axis=1), 0)
    own_ids = jnp.broadcast_to(jnp.arange(RB, dtype=jnp.int32)[None, :], (PARTS_SIZE, RB))
    offset = jax.random.randint(keys[4], (PARTS_SIZE, RB), 1, RB)
    local_row = jnp.concatenate([own_ids, own_ids], axis=1)
    local_col = jnp.concatenate([own_ids, (own_ids + offset) % RB], axis=1)
    tile_row = jnp.concatenate([local_row, remote_row], axis=1).astype(jnp.int32)
    tile_col = jnp.concatenate([local_col, remote_col], axis=1).astype(jnp.int32)
    tile_count = (2 * RB + jnp.sum(multiple, axis=1)).astype(jnp.int32)
    return (tile_row, tile_col, tile_count, send_block.astype(jnp.int32))


def draw_tile_row(key, part):
    return graph_tables(key)[0]


def draw_tile_col(key, part):
    return graph_tables(key)[1]


def draw_tile_count(key, part):
    return graph_tables(key)[2]


def draw_send_block(key, part):
    return graph_tables(key)[3]


def with_ends(values, own_key, least, top_value):
    place = [jax.random.randint(jax.random.fold_in(own_key, axis), (), 0, length) for axis, length in enumerate(values.shape)]
    widest = values.shape.index(max(values.shape))
    next_to = place[:widest] + [(place[widest] + 1) % values.shape[widest]] + place[widest + 1:]
    return values.at[tuple(place)].set(least).at[tuple(next_to)].set(top_value)


def raised(entries, stream_key, source, target, parts, factor):
    def block_of(axis_at):
        return (jnp.arange(entries.shape[axis_at]) // (entries.shape[axis_at] // parts)).reshape((-1,) + (1,) * (entries.ndim - 1 - axis_at))

    one_side = jax.random.permutation(stream_key, parts)[block_of(target)]
    second = (block_of(target) + parts // 2) % parts
    return jnp.where((block_of(source) == one_side) | (block_of(source) == second), factor * entries, entries)


def block_scale(rng, extent, cuts, low, high):
    def one(dim, shards_of):
        draws = jax.random.uniform(jax.random.fold_in(jax.random.fold_in(rng, 6), dim), (shards_of,), jnp.float32, low / len(cuts), high / len(cuts))
        return jnp.repeat(jnp.exp(draws), extent[dim] // shards_of).reshape((-1,) + (1,) * (len(extent) - dim - 1))

    level = one(*cuts[0])
    for cut in cuts[1:]:
        level = level * one(*cut)
    return level


def bell_draw(key, extent, scale, limit, pieces=(), kind=jnp.bfloat16):
    entries = scale * jax.random.normal(key, extent, jnp.float32)
    if pieces:
        entries = entries * block_scale(key, extent, pieces, -0.22, 0.18)
    return jnp.clip(entries, -limit, limit).astype(kind)


def noise_with(stream_key, shape, scale, bound, shards, heavy, held_as=jnp.bfloat16):
    values = scale * jax.random.normal(stream_key, shape, jnp.float32)
    if shards:
        values = values * block_scale(stream_key, shape, shards, -0.22, 0.18)
    return jnp.clip(raised(values, jax.random.fold_in(stream_key, 3), *heavy), -bound, bound).astype(held_as)


def setup_inputs(seed: int = 0) -> dict:
    key_of = jax.random.split(jax.random.key(seed), 11)
    return {
        "features": bell_draw(key_of[0], (NODES, F), 1.0, 6.0, ((0, 8), (1, 4)), jnp.float32),
        "degrees": with_ends(jax.random.randint(key_of[1], (NODES,), 1, 5), jax.random.fold_in(key_of[1], 1), 1, 4).astype(jnp.int32),
        "tile_row": draw_tile_row(jax.random.fold_in(key_of[10], 71), 0),
        "tile_col": draw_tile_col(jax.random.fold_in(key_of[10], 71), 0),
        "tile_count": draw_tile_count(jax.random.fold_in(key_of[10], 71), 0),
        "send_block": draw_send_block(jax.random.fold_in(key_of[10], 71), 0),
        "tile_val": bell_draw(key_of[6], (PARTS_SIZE, TILES_DEV, BLOCK, BLOCK), (2 * RB * BLOCK) ** -0.5, 0.15625, ((0, 8),)),
        "weight": bell_draw(key_of[7], (OUT, HOPS + 1, F), ((HOPS + 1) * F) ** -0.5, 0.109375, ((0, 8), (2, 4))),
        "out_bias": bell_draw(key_of[8], (OUT,), 0.5, 3.0, (), jnp.float32),
        "cotangent": noise_with(key_of[9], (NODES, OUT), (NODES ** -0.5), 0.076171875, ((0, 32),), (0, 1, 32, 2.75)),
    }


def hop_product(source_blocks, tile_row, tile_col, tile_val, tile_count, send_block):
    part_ids = jnp.arange(PARTS_SIZE, dtype=jnp.int32)
    block_ids = jnp.arange(RB, dtype=jnp.int32)

    def one_part(items):
        part, row_ids, col_ids, values, live_count, received = items
        sender = jnp.clip(col_ids - RB, 0, PARTS_SIZE - 1).astype(jnp.int32)
        global_col = jnp.where(col_ids < RB, part * RB + col_ids, sender * RB + received[sender]).astype(jnp.int32)
        picked = source_blocks[global_col].astype(jnp.float32)
        product = jnp.einsum('tij,tjc->tic', values.astype(jnp.float32), picked)
        is_live = jnp.arange(row_ids.shape[0], dtype=jnp.int32) < live_count
        onehot = ((row_ids[:, None] == block_ids[None, :]) & is_live[:, None]).astype(jnp.float32)
        return jnp.einsum('tr,tic->ric', onehot, product, precision=lax.Precision.HIGHEST)
    return lax.map(one_part, (part_ids, tile_row, tile_col, tile_val, tile_count, send_block.T))

def reference(features, degrees, tile_row, tile_col, tile_count, send_block, tile_val, weight, out_bias, cotangent):
    row_scale = lax.rsqrt(degrees.astype(jnp.float32))[:, None]
    source = (features * row_scale).astype(jnp.bfloat16)
    hop_list = [features.astype(jnp.bfloat16)]
    for hop_number in range(HOPS):
        summed = hop_product(source.reshape(NBLOCKS, BLOCK, F), tile_row, tile_col, tile_val, tile_count, send_block)
        summed = summed.reshape(NODES, F)
        hop_list.append((summed * row_scale).astype(jnp.bfloat16))
        if hop_number + 1 < HOPS:
            source = (summed * row_scale * row_scale).astype(jnp.bfloat16)
    stacked = jnp.stack(hop_list, axis=1).reshape(NODES, (HOPS + 1) * F)
    flat_weight = weight.reshape(OUT, (HOPS + 1) * F)
    linear = lax.dot_general(stacked, flat_weight, (((1,), (1,)), ((), ())), preferred_element_type=jnp.float32)
    linear = linear + out_bias[None, :]
    sigmoid_val = jax.nn.sigmoid(linear)
    output = (linear * sigmoid_val).astype(jnp.bfloat16)
    grad_linear = (cotangent.astype(jnp.float32) * sigmoid_val * (1.0 + linear * (1.0 - sigmoid_val))).astype(jnp.bfloat16)
    weight_grad = lax.dot_general(grad_linear, stacked, (((0,), (0,)), ((), ())), preferred_element_type=jnp.float32)
    weight_grad = weight_grad.reshape(OUT, HOPS + 1, F)
    bias_grad = lax.optimization_barrier(jnp.sum(grad_linear.astype(jnp.float32), axis=0))
    return (output, weight_grad, bias_grad)
```

```python
import functools

import jax
import jax.numpy as jnp
from jax import lax
from jax.experimental import pallas as pl
from jax.experimental.pallas import tpu as pltpu
from jax.sharding import PartitionSpec as P

HOPS = 2
PIECES = 2
MESH = pl.DeviceIdType.MESH


def matrix_kernel(tile_row, tile_col, tile_count, tile_val, matrix):
    block = tile_val.shape[-1]
    matrix[...] = jnp.zeros_like(matrix)

    def place(tile, carry):
        row = pl.multiple_of(tile_row[0, tile] * block, block)
        col = pl.multiple_of(tile_col[0, tile] * block, block)
        here = (pl.ds(row, block), pl.ds(col, block))
        total = matrix[here].astype(jnp.float32) + tile_val[0, tile].astype(jnp.float32)
        matrix[here] = total.astype(jnp.bfloat16)
        return carry

    lax.fori_loop(0, tile_count[0], place, 0)


def dense_matrix(tile_row, tile_col, tile_count, tile_val, own_nodes):
    block = tile_val.shape[-1]
    columns = own_nodes + lax.axis_size("node") * block
    smem = pl.BlockSpec(memory_space=pltpu.SMEM)
    vmem = pl.BlockSpec(memory_space=pltpu.VMEM)
    return pl.pallas_call(
        matrix_kernel,
        out_shape=jax.ShapeDtypeStruct((own_nodes, columns), jnp.bfloat16),
        in_specs=[smem, smem, smem, vmem],
        out_specs=vmem,
        compiler_params=pltpu.CompilerParams(vmem_limit_bytes=40 * 1024 * 1024),
        name="matrix",
    )(tile_row, tile_col, tile_count, tile_val)


def hops_kernel(
    nodes, send_block, features, scale, matrix, rows, source, outgoing, frame, acc, s_sem, r_sem
):
    node = lax.axis_index("node")
    feat = lax.axis_index("feat")
    own_nodes, panel = features.shape
    block = frame.shape[2]
    barrier = pltpu.get_barrier_semaphore()
    for hop in range(1, nodes):
        pl.semaphore_signal(
            barrier, inc=1, device_id=(lax.rem(node + hop, nodes), feat), device_id_type=MESH
        )

    def put_source(values):
        source[...] = values.astype(jnp.bfloat16).reshape(source.shape)

    put_source(features[...] * scale[...])
    rows[:, pl.ds(0, panel)] = features[...].astype(jnp.bfloat16)
    pl.semaphore_wait(barrier, nodes - 1)

    group = min(nodes, 8)
    copies = []
    for step in range(HOPS):
        arrivals = []
        for hop in range(1, nodes):
            part = lax.rem(node + hop, nodes)
            outgoing[step, hop - 1] = source[send_block[node, part]]
            copy = pltpu.make_async_remote_copy(
                src_ref=outgoing.at[step, hop - 1],
                dst_ref=frame.at[step, node],
                send_sem=s_sem.at[step, hop - 1],
                recv_sem=r_sem.at[step, hop - 1],
                device_id=(part, feat),
                device_id_type=MESH,
            )
            copy.start()
            copies.append(copy)
            sender = lax.rem(node + nodes - hop, nodes)
            arrivals.append(
                pltpu.make_async_remote_copy(
                    src_ref=outgoing.at[step, hop - 1],
                    dst_ref=frame.at[step, sender],
                    send_sem=s_sem.at[step, hop - 1],
                    recv_sem=r_sem.at[step, hop - 1],
                    device_id=(part, feat),
                    device_id_type=MESH,
                )
            )
        frame[step, node] = jnp.zeros((block, panel), jnp.bfloat16)
        acc[...] = jnp.dot(
            matrix[:, pl.ds(0, own_nodes)],
            source[...].reshape(own_nodes, panel),
            preferred_element_type=jnp.float32,
        )
        for arrival in arrivals:
            arrival.wait_recv()

        def add(first):
            start = pl.multiple_of(own_nodes + first * block, block)
            acc[...] += jnp.dot(
                matrix[:, pl.ds(start, group * block)],
                frame[step, pl.ds(first, group)].reshape(group * block, panel),
                preferred_element_type=jnp.float32,
            )

        if nodes == group:
            add(0)
        else:

            def add_group(index, carry):
                add(index * group)
                return carry

            lax.fori_loop(0, nodes // group, add_group, 0)
        hop_value = acc[...] * scale[...]
        rows[:, pl.ds((step + 1) * panel, panel)] = hop_value.astype(jnp.bfloat16)
        if step + 1 < HOPS:
            put_source(hop_value * scale[...])
    for copy in copies:
        copy.wait_send()


def hops(features, scale, matrix, send_block, block):
    nodes = lax.axis_size("node")
    own_nodes, panel = features.shape
    smem = pl.BlockSpec(memory_space=pltpu.SMEM)
    vmem = pl.BlockSpec(memory_space=pltpu.VMEM)
    dma = pltpu.SemaphoreType.DMA
    return pl.pallas_call(
        functools.partial(hops_kernel, nodes),
        out_shape=jax.ShapeDtypeStruct((own_nodes, (HOPS + 1) * panel), jnp.bfloat16),
        in_specs=[smem, vmem, vmem, vmem],
        out_specs=vmem,
        scratch_shapes=[
            pltpu.VMEM((own_nodes // block, block, panel), jnp.bfloat16),
            pltpu.VMEM((HOPS, nodes - 1, block, panel), jnp.bfloat16),
            pltpu.VMEM((HOPS, nodes, block, panel), jnp.bfloat16),
            pltpu.VMEM((own_nodes, panel), jnp.float32),
            dma((HOPS, nodes - 1)),
            dma((HOPS, nodes - 1)),
        ],
        compiler_params=pltpu.CompilerParams(
            collective_id=1, has_side_effects=True, vmem_limit_bytes=48 * 1024 * 1024
        ),
        cost_estimate=pl.CostEstimate(
            flops=HOPS * 2 * matrix.shape[0] * matrix.shape[1] * panel,
            bytes_accessed=100 * 1024 * 1024,
            transcendentals=0,
        ),
        name="hops",
    )(send_block, features, scale, matrix)


def layer_kernel(
    nodes,
    feats,
    rows_ref,
    weight_ref,
    bias_ref,
    cot_ref,
    out_ref,
    wgrad_ref,
    bgrad_ref,
    pair_send,
    pair_recv,
    held,
    far_send,
    far_recv,
    grad_all,
    block,
    x_send,
    x_recv,
    x_held,
    z_send,
    z_recv,
    bias_all,
    pair_s,
    pair_r,
    far_s,
    far_r,
    gpair_s,
    gpair_r,
    gfar_s,
    gfar_r,
    gfwd_s,
    gfwd_r,
    x_s,
    x_r,
    z_s,
    z_r,
    b_s,
    b_r,
):
    node = lax.axis_index("node")
    feat = lax.axis_index("feat")
    side, high = lax.rem(feat, 2), feat // 2
    highs = feats // 2
    lane, depth = lax.rem(node, 2), node // 2
    depths = nodes // 2
    own_rows = cot_ref.shape[0]
    piece = own_rows // PIECES
    units = wgrad_ref.shape[0]
    pair_feat = feat + 1 - 2 * side

    def far_high(step):
        return lax.rem(high + 1 + step, highs)

    def far_depth(step):
        return lax.rem(depth + 1 + step, depths)

    barrier = pltpu.get_barrier_semaphore()
    pl.semaphore_signal(barrier, inc=1, device_id=(node, pair_feat), device_id_type=MESH)
    for step in range(highs - 1):
        pl.semaphore_signal(
            barrier, inc=1, device_id=(node, far_high(step) * 2 + side), device_id_type=MESH
        )
    for step in range(1, nodes):
        pl.semaphore_signal(
            barrier, inc=1, device_id=(lax.rem(node + step, nodes), feat), device_id_type=MESH
        )
    pl.semaphore_wait(barrier, highs + nodes - 1)

    def terms(owner, part):
        start = pl.multiple_of(owner * own_rows + part * piece, 16)
        return lax.dot_general(
            rows_ref[pl.ds(start, piece), :],
            weight_ref[...],
            (((1,), (1,)), ((), ())),
            preferred_element_type=jnp.float32,
        )

    def remote(src, dst, s, r, device):
        return pltpu.make_async_remote_copy(
            src_ref=src,
            dst_ref=dst,
            send_sem=s,
            recv_sem=r,
            device_id=device,
            device_id_type=MESH,
        )

    pair = (node, pair_feat)
    sends = []
    far_copies = {}
    for step in range(highs):
        for part in range(PIECES):
            slot = step * PIECES + part
            owner = far_high(step) * 2
            pair_send[slot] = terms(owner + 1 - side, part)
            copy = remote(
                pair_send.at[slot], pair_recv.at[slot], pair_s.at[slot], pair_r.at[slot], pair
            )
            copy.start()
            own = terms(owner + side, part)
            copy.wait()
            total = own + pair_recv[slot]
            if step < highs - 1:
                far_send[slot] = total.astype(jnp.bfloat16)
                far = remote(
                    far_send.at[slot],
                    far_recv.at[slot],
                    far_s.at[slot],
                    far_r.at[slot],
                    (node, owner + side),
                )
                far.start()
                far_copies[slot] = far
            else:
                held[part] = total

    def grad_rows(owner, part):
        return pl.ds(pl.multiple_of(owner * own_rows + part * piece, 16), piece)

    for part in range(PIECES):
        linear = held[part]
        for step in range(highs - 1):
            slot = step * PIECES + part
            far_copies[slot].wait()
            linear = linear + far_recv[slot].astype(jnp.float32)
        linear = linear + bias_ref[...]
        gate = 1.0 / (1.0 + jnp.exp(-linear))
        window = pl.ds(part * piece, piece)
        out_ref[window, :] = (linear * gate).astype(jnp.bfloat16)
        grad = cot_ref[window, :].astype(jnp.float32) * gate * (1.0 + linear * (1.0 - gate))
        mine = grad_rows(feat, part)
        grad_all[mine, :] = grad.astype(jnp.bfloat16)
        for step in range(highs - 1):
            slot = step * PIECES + part
            far = remote(
                grad_all.at[mine, :],
                grad_all.at[mine, :],
                gfar_s.at[slot],
                gfar_r.at[slot],
                (node, far_high(step) * 2 + side),
            )
            far.start()
            sends.append(far)
        near = remote(
            grad_all.at[mine, :], grad_all.at[mine, :], gpair_s.at[part], gpair_r.at[part], pair
        )
        near.start()
        sends.append(near)

    forwards = []
    for part in range(PIECES):
        for step in range(highs - 1):
            slot = step * PIECES + part
            origin = lax.rem(high + highs - 1 - step, highs) * 2 + side
            theirs = grad_rows(origin, part)
            remote(
                grad_all.at[theirs, :],
                grad_all.at[theirs, :],
                gfar_s.at[slot],
                gfar_r.at[slot],
                pair,
            ).wait_recv()
            forward = remote(
                grad_all.at[theirs, :],
                grad_all.at[theirs, :],
                gfwd_s.at[slot],
                gfwd_r.at[slot],
                pair,
            )
            forward.start()
            forwards.append(forward)
    for part in range(PIECES):
        other = grad_rows(pair_feat, part)
        remote(
            grad_all.at[other, :], grad_all.at[other, :], gpair_s.at[part], gpair_r.at[part], pair
        ).wait_recv()
        for step in range(highs - 1):
            slot = step * PIECES + part
            origin = lax.rem(high + highs - 1 - step, highs) * 2 + 1 - side
            theirs = grad_rows(origin, part)
            remote(
                grad_all.at[theirs, :],
                grad_all.at[theirs, :],
                gfwd_s.at[slot],
                gfwd_r.at[slot],
                pair,
            ).wait_recv()

    x_pair = (node + 1 - 2 * lane, feat)
    x_copies = []
    z_copies = []

    def finish(step):
        x_copies[step].wait()
        total = x_held[step] + x_recv[step].astype(jnp.float32)
        if step < depths - 1:
            z_send[step] = total.astype(jnp.bfloat16)
            copy = remote(
                z_send.at[step],
                z_recv.at[step],
                z_s.at[step],
                z_r.at[step],
                (far_depth(step) * 2 + lane, feat),
            )
            copy.start()
            z_copies.append(copy)
        else:
            wgrad_ref[...] = total

    def weight_terms(start, count):
        return lax.dot_general(
            grad_all[:, pl.ds(start, count)],
            rows_ref[...],
            (((0,), (0,)), ((), ())),
            preferred_element_type=jnp.float32,
        )

    outs = grad_all.shape[1]
    aligned = (2 * units) % 128 == 0
    if not aligned:
        for start in range(0, outs, 128):
            block[pl.ds(start, 128), :] = weight_terms(start, 128)

    b_copies = []
    for step in range(depths):
        start = pl.multiple_of(far_depth(step) * (2 * units), 2 * units)
        if aligned:
            block[...] = weight_terms(start, 2 * units)
            start = 0
        theirs = pl.ds(pl.multiple_of(start + (1 - lane) * units, 16), units)
        mine = pl.ds(pl.multiple_of(start + lane * units, 16), units)
        x_send[step] = block[theirs, :].astype(jnp.bfloat16)
        copy = remote(x_send.at[step], x_recv.at[step], x_s.at[step], x_r.at[step], x_pair)
        copy.start()
        x_copies.append(copy)
        x_held[step] = block[mine, :]
        if step == 0:
            bias_all[node] = jnp.sum(grad_all[...].astype(jnp.float32), axis=0, keepdims=True)
            for hop in range(1, nodes):
                copy = remote(
                    bias_all.at[node],
                    bias_all.at[node],
                    b_s.at[hop - 1],
                    b_r.at[hop - 1],
                    (lax.rem(node + hop, nodes), feat),
                )
                copy.start()
                b_copies.append(copy)
        else:
            finish(step - 1)
    finish(depths - 1)

    for hop in range(1, nodes):
        sender = lax.rem(node + nodes - hop, nodes)
        remote(
            bias_all.at[sender],
            bias_all.at[sender],
            b_s.at[hop - 1],
            b_r.at[hop - 1],
            (lax.rem(node + hop, nodes), feat),
        ).wait_recv()
    bias_total = bias_all[0]
    for part in range(1, nodes):
        bias_total = bias_total + bias_all[part]
    bgrad_ref[...] = bias_total

    for step in range(depths - 1):
        z_copies[step].wait()
        wgrad_ref[...] += z_recv[step].astype(jnp.float32)
    for copy in sends + forwards + b_copies:
        copy.wait_send()


def layer(rows, flat_weight, out_bias, cotangent):
    nodes, feats = lax.axis_size("node"), lax.axis_size("feat")
    highs, depths = feats // 2, nodes // 2
    total_rows, width = rows.shape
    outs = flat_weight.shape[0]
    own_rows = cotangent.shape[0]
    units = outs // nodes
    piece = own_rows // PIECES
    block_rows = 2 * units if (2 * units) % 128 == 0 else outs
    slots = highs * PIECES
    far_slots = max(1, (highs - 1) * PIECES)
    z_slots = max(1, depths - 1)
    dma = pltpu.SemaphoreType.DMA
    vmem = pl.BlockSpec(memory_space=pltpu.VMEM)
    flops = 4 * total_rows * width * outs
    return pl.pallas_call(
        functools.partial(layer_kernel, nodes, feats),
        out_shape=(
            jax.ShapeDtypeStruct((own_rows, outs), jnp.bfloat16),
            jax.ShapeDtypeStruct((units, width), jnp.float32),
            jax.ShapeDtypeStruct((1, outs), jnp.float32),
        ),
        in_specs=[vmem] * 4,
        out_specs=(vmem,) * 3,
        scratch_shapes=[
            pltpu.VMEM((slots, piece, outs), jnp.float32),
            pltpu.VMEM((slots, piece, outs), jnp.float32),
            pltpu.VMEM((PIECES, piece, outs), jnp.float32),
            pltpu.VMEM((far_slots, piece, outs), jnp.bfloat16),
            pltpu.VMEM((far_slots, piece, outs), jnp.bfloat16),
            pltpu.VMEM((total_rows, outs), jnp.bfloat16),
            pltpu.VMEM((block_rows, width), jnp.float32),
            pltpu.VMEM((depths, units, width), jnp.bfloat16),
            pltpu.VMEM((depths, units, width), jnp.bfloat16),
            pltpu.VMEM((depths, units, width), jnp.float32),
            pltpu.VMEM((z_slots, units, width), jnp.bfloat16),
            pltpu.VMEM((z_slots, units, width), jnp.bfloat16),
            pltpu.VMEM((nodes, 1, outs), jnp.float32),
            dma((slots,)),
            dma((slots,)),
            dma((far_slots,)),
            dma((far_slots,)),
            dma((PIECES,)),
            dma((PIECES,)),
            dma((far_slots,)),
            dma((far_slots,)),
            dma((far_slots,)),
            dma((far_slots,)),
            dma((depths,)),
            dma((depths,)),
            dma((z_slots,)),
            dma((z_slots,)),
            dma((nodes,)),
            dma((nodes,)),
        ],
        compiler_params=pltpu.CompilerParams(
            collective_id=0, has_side_effects=True, vmem_limit_bytes=48 * 1024 * 1024
        ),
        cost_estimate=pl.CostEstimate(
            flops=flops, bytes_accessed=8 * total_rows * outs, transcendentals=own_rows * outs
        ),
        name="layer",
    )(rows, flat_weight, out_bias[None, :], cotangent)


def local(
    features,
    degrees,
    tile_row,
    tile_col,
    tile_count,
    send_block,
    tile_val,
    weight,
    out_bias,
    cotangent,
):
    row_scale = lax.rsqrt(degrees.astype(jnp.float32))[:, None]
    flat_weight = lax.all_gather(weight.reshape(weight.shape[0], -1), "node", axis=0, tiled=True)
    matrix = dense_matrix(tile_row, tile_col, tile_count, tile_val, features.shape[0])
    rows = hops(features, row_scale, matrix, send_block, tile_val.shape[-1])
    output, weight_grad, bias_grad = layer(rows, flat_weight, out_bias, cotangent)
    return (output, weight_grad.reshape(weight.shape), bias_grad[0])


def solution(mesh):
    in_specs = (
        P("node", "feat"),
        P("node"),
        P("node", None),
        P("node", None),
        P("node"),
        P(),
        P("node", None, None, None),
        P("node", None, "feat"),
        P(),
        P(("node", "feat"), None),
    )
    out_specs = (P(("node", "feat"), None), P("node", None, "feat"), P())
    return jax.shard_map(local, mesh=mesh, in_specs=in_specs, out_specs=out_specs, check_vma=False)
```

```python
import functools

import jax
import jax.numpy as jnp
from jax import lax
from jax.experimental import pallas as pl
from jax.experimental.pallas import tpu as pltpu
from jax.sharding import PartitionSpec as P

HOPS = 2
MESH = pl.DeviceIdType.MESH


def matrix_kernel(tile_row, tile_col, tile_count, tile_val, matrix):
    block = tile_val.shape[-1]
    matrix[...] = jnp.zeros_like(matrix)

    def place(tile, carry):
        row = pl.multiple_of(tile_row[0, tile] * block, block)
        col = pl.multiple_of(tile_col[0, tile] * block, block)
        here = (pl.ds(row, block), pl.ds(col, block))
        total = matrix[here].astype(jnp.float32) + tile_val[0, tile].astype(jnp.float32)
        matrix[here] = total.astype(jnp.bfloat16)
        return carry

    lax.fori_loop(0, tile_count[0], place, 0)


def dense_matrix(tile_row, tile_col, tile_count, tile_val, own_nodes):
    block = tile_val.shape[-1]
    columns = own_nodes + lax.axis_size("node") * block
    smem = pl.BlockSpec(memory_space=pltpu.SMEM)
    vmem = pl.BlockSpec(memory_space=pltpu.VMEM)
    return pl.pallas_call(
        matrix_kernel,
        out_shape=jax.ShapeDtypeStruct((own_nodes, columns), jnp.bfloat16),
        in_specs=[smem, smem, smem, vmem],
        out_specs=vmem,
        compiler_params=pltpu.CompilerParams(vmem_limit_bytes=40 * 1024 * 1024),
        name="matrix",
    )(tile_row, tile_col, tile_count, tile_val)


def hops_kernel(
    nodes, send_block, features, scale, matrix, rows, source, outgoing, frame, acc, s_sem, r_sem
):
    node = lax.axis_index("node")
    feat = lax.axis_index("feat")
    own_nodes, panel = features.shape
    block = frame.shape[2]
    barrier = pltpu.get_barrier_semaphore()
    for hop in range(1, nodes):
        pl.semaphore_signal(
            barrier, inc=1, device_id=(lax.rem(node + hop, nodes), feat), device_id_type=MESH
        )

    def put_source(values):
        source[...] = values.astype(jnp.bfloat16).reshape(source.shape)

    put_source(features[...] * scale[...])
    rows[:, pl.ds(0, panel)] = features[...].astype(jnp.bfloat16)
    pl.semaphore_wait(barrier, nodes - 1)

    group = min(nodes, 8)
    copies = []
    for step in range(HOPS):
        arrivals = []
        for hop in range(1, nodes):
            part = lax.rem(node + hop, nodes)
            outgoing[step, hop - 1] = source[send_block[node, part]]
            copy = pltpu.make_async_remote_copy(
                src_ref=outgoing.at[step, hop - 1],
                dst_ref=frame.at[step, node],
                send_sem=s_sem.at[step, hop - 1],
                recv_sem=r_sem.at[step, hop - 1],
                device_id=(part, feat),
                device_id_type=MESH,
            )
            copy.start()
            copies.append(copy)
            sender = lax.rem(node + nodes - hop, nodes)
            arrivals.append(
                pltpu.make_async_remote_copy(
                    src_ref=outgoing.at[step, hop - 1],
                    dst_ref=frame.at[step, sender],
                    send_sem=s_sem.at[step, hop - 1],
                    recv_sem=r_sem.at[step, hop - 1],
                    device_id=(part, feat),
                    device_id_type=MESH,
                )
            )
        frame[step, node] = jnp.zeros((block, panel), jnp.bfloat16)
        acc[...] = jnp.dot(
            matrix[:, pl.ds(0, own_nodes)],
            source[...].reshape(own_nodes, panel),
            preferred_element_type=jnp.float32,
        )
        for arrival in arrivals:
            arrival.wait_recv()

        def add(first):
            start = pl.multiple_of(own_nodes + first * block, block)
            acc[...] += jnp.dot(
                matrix[:, pl.ds(start, group * block)],
                frame[step, pl.ds(first, group)].reshape(group * block, panel),
                preferred_element_type=jnp.float32,
            )

        if nodes == group:
            add(0)
        else:

            def add_group(index, carry):
                add(index * group)
                return carry

            lax.fori_loop(0, nodes // group, add_group, 0)
        hop_value = acc[...] * scale[...]
        rows[:, pl.ds((step + 1) * panel, panel)] = hop_value.astype(jnp.bfloat16)
        if step + 1 < HOPS:
            put_source(hop_value * scale[...])
    for copy in copies:
        copy.wait_send()


def hops(features, scale, matrix, send_block, block):
    nodes = lax.axis_size("node")
    own_nodes, panel = features.shape
    smem = pl.BlockSpec(memory_space=pltpu.SMEM)
    vmem = pl.BlockSpec(memory_space=pltpu.VMEM)
    dma = pltpu.SemaphoreType.DMA
    return pl.pallas_call(
        functools.partial(hops_kernel, nodes),
        out_shape=jax.ShapeDtypeStruct((own_nodes, (HOPS + 1) * panel), jnp.bfloat16),
        in_specs=[smem, vmem, vmem, vmem],
        out_specs=vmem,
        scratch_shapes=[
            pltpu.VMEM((own_nodes // block, block, panel), jnp.bfloat16),
            pltpu.VMEM((HOPS, nodes - 1, block, panel), jnp.bfloat16),
            pltpu.VMEM((HOPS, nodes, block, panel), jnp.bfloat16),
            pltpu.VMEM((own_nodes, panel), jnp.float32),
            dma((HOPS, nodes - 1)),
            dma((HOPS, nodes - 1)),
        ],
        compiler_params=pltpu.CompilerParams(
            collective_id=1, has_side_effects=True, vmem_limit_bytes=48 * 1024 * 1024
        ),
        cost_estimate=pl.CostEstimate(
            flops=HOPS * 2 * matrix.shape[0] * matrix.shape[1] * panel,
            bytes_accessed=100 * 1024 * 1024,
            transcendentals=0,
        ),
        name="hops",
    )(send_block, features, scale, matrix)


def layer_kernel(
    nodes,
    feats,
    cols,
    rows_ref,
    weight_ref,
    bias_ref,
    cot_ref,
    out_ref,
    wgrad_ref,
    bgrad_ref,
    terms,
    pair_recv,
    held,
    far_send,
    far_recv,
    grad_all,
    block,
    x_send,
    x_recv,
    x_held,
    z_send,
    z_recv,
    bias_all,
    pair_s,
    pair_r,
    far_s,
    far_r,
    gpair_s,
    gpair_r,
    gfar_s,
    gfar_r,
    gfwd_s,
    gfwd_r,
    x_s,
    x_r,
    z_s,
    z_r,
    b_s,
    b_r,
):
    node = lax.axis_index("node")
    feat = lax.axis_index("feat")
    side, high = lax.rem(feat, 2), feat // 2
    highs = feats // 2
    lane, depth = lax.rem(node, 2), node // 2
    own_rows = cot_ref.shape[0]
    units = wgrad_ref.shape[0]
    pieces = weight_ref.shape[0] // cols
    share = cols // (2 * units)
    pair = (node, feat + 1 - 2 * side)
    x_pair = (node + 1 - 2 * lane, feat)

    def far_feat(step):
        return lax.rem(high + 1 + step, highs) * 2 + side

    def window(index):
        piece = lax.rem(depth // share + 1 + index, pieces)
        return pl.ds(pl.multiple_of(piece * cols, cols), cols)

    def target(index, sub):
        piece = lax.rem(depth // share + 1 + index, pieces)
        return piece * share + lax.rem(lax.rem(depth, share) + 1 + sub, share)

    def chunk(owner):
        return pl.ds(pl.multiple_of(owner * own_rows, 16), own_rows)

    def remote(src, dst, s, r, device):
        return pltpu.make_async_remote_copy(
            src_ref=src,
            dst_ref=dst,
            send_sem=s,
            recv_sem=r,
            device_id=device,
            device_id_type=MESH,
        )

    barrier = pltpu.get_barrier_semaphore()
    pl.semaphore_signal(barrier, inc=1, device_id=pair, device_id_type=MESH)
    for step in range(highs - 1):
        pl.semaphore_signal(
            barrier, inc=1, device_id=(node, far_feat(step)), device_id_type=MESH
        )
    for step in range(1, nodes):
        pl.semaphore_signal(
            barrier, inc=1, device_id=(lax.rem(node + step, nodes), feat), device_id_type=MESH
        )

    started = []
    pair_copies = {}
    far_copies = {}
    near_grads = {}
    far_grads = {}
    x_copies = {}
    z_copies = []

    def make_terms(index):
        terms[index] = lax.dot_general(
            rows_ref[...],
            weight_ref[window(index), :],
            (((1,), (1,)), ((), ())),
            preferred_element_type=jnp.float32,
        )
        if index == 0:
            pl.semaphore_wait(barrier, highs + nodes - 1)
        for top in range(highs):
            copy = remote(
                terms.at[index, chunk(top * 2 + 1 - side), :],
                pair_recv.at[index, top],
                pair_s.at[index, top],
                pair_r.at[index, top],
                pair,
            )
            copy.start()
            pair_copies[index, top] = copy

    def add_pair(index):
        for top in range(highs):
            pair_copies[index, top].wait()
        for step in range(highs - 1):
            owner = far_feat(step)
            total = terms[index, chunk(owner), :] + pair_recv[index, owner // 2]
            far_send[index, step] = total.astype(jnp.bfloat16)
            copy = remote(
                far_send.at[index, step],
                far_recv.at[index, step],
                far_s.at[index, step],
                far_r.at[index, step],
                (node, owner),
            )
            copy.start()
            far_copies[index, step] = copy
        held[index] = terms[index, chunk(feat), :] + pair_recv[index, high]

    def make_grad(index):
        linear = held[index]
        for step in range(highs - 1):
            far_copies[index, step].wait()
            linear = linear + far_recv[index, step].astype(jnp.float32)
        linear = linear + bias_ref[:, window(index)]
        gate = 1.0 / (1.0 + jnp.exp(-linear))
        out_ref[:, window(index)] = (linear * gate).astype(jnp.bfloat16)
        slope = gate * (1.0 + linear * (1.0 - gate))
        grad = cot_ref[:, window(index)].astype(jnp.float32) * slope
        grad_all[index, chunk(feat), :] = grad.astype(jnp.bfloat16)
        mine = grad_all.at[index, chunk(feat), :]
        for step in range(highs - 1):
            copy = remote(
                mine, mine, gfar_s.at[index, step], gfar_r.at[index, step], (node, far_feat(step))
            )
            copy.start()
            started.append(copy)
        copy = remote(mine, mine, gpair_s.at[index], gpair_r.at[index], pair)
        copy.start()
        started.append(copy)

    def forward_grad(index):
        for step in range(highs - 1):
            origin = lax.rem(high + highs - 1 - step, highs) * 2 + side
            theirs = grad_all.at[index, chunk(origin), :]
            remote(
                theirs, theirs, gfar_s.at[index, step], gfar_r.at[index, step], pair
            ).wait_recv()
            copy = remote(theirs, theirs, gfwd_s.at[index, step], gfwd_r.at[index, step], pair)
            copy.start()
            started.append(copy)

    def weight_terms(index):
        other = grad_all.at[index, chunk(feat + 1 - 2 * side), :]
        remote(other, other, gpair_s.at[index], gpair_r.at[index], pair).wait_recv()
        for step in range(highs - 1):
            origin = lax.rem(high + highs - 1 - step, highs) * 2 + 1 - side
            theirs = grad_all.at[index, chunk(origin), :]
            remote(
                theirs, theirs, gfwd_s.at[index, step], gfwd_r.at[index, step], pair
            ).wait_recv()
        block[...] = lax.dot_general(
            grad_all[index],
            rows_ref[...],
            (((0,), (0,)), ((), ())),
            preferred_element_type=jnp.float32,
        )
        for sub in range(share):
            slot = index * share + sub
            start = lax.rem(lax.rem(depth, share) + 1 + sub, share) * (2 * units)
            theirs = pl.ds(pl.multiple_of(start + (1 - lane) * units, 16), units)
            mine = pl.ds(pl.multiple_of(start + lane * units, 16), units)
            x_send[slot] = block[theirs, :].astype(jnp.bfloat16)
            copy = remote(x_send.at[slot], x_recv.at[slot], x_s.at[slot], x_r.at[slot], x_pair)
            copy.start()
            x_copies[slot] = copy
            x_held[slot] = block[mine, :]
        bias_all[node, :, window(index)] = jnp.sum(
            grad_all[index].astype(jnp.float32), axis=0, keepdims=True
        )
        if index == pieces - 1:
            for hop in range(1, nodes):
                copy = remote(
                    bias_all.at[node],
                    bias_all.at[node],
                    b_s.at[hop - 1],
                    b_r.at[hop - 1],
                    (lax.rem(node + hop, nodes), feat),
                )
                copy.start()
                started.append(copy)

    def add_x(index):
        for sub in range(share):
            slot = index * share + sub
            x_copies[slot].wait()
            total = x_held[slot] + x_recv[slot].astype(jnp.float32)
            if slot == pieces * share - 1:
                wgrad_ref[...] = total
                continue
            z_send[slot] = total.astype(jnp.bfloat16)
            copy = remote(
                z_send.at[slot],
                z_recv.at[slot],
                z_s.at[slot],
                z_r.at[slot],
                (target(index, sub) * 2 + lane, feat),
            )
            copy.start()
            z_copies.append(copy)

    stages = (make_terms, add_pair, make_grad, forward_grad, weight_terms, add_x)
    for tick in range(pieces + len(stages) - 1):
        for order, stage in enumerate(stages):
            if 0 <= tick - order < pieces:
                stage(tick - order)

    for hop in range(1, nodes):
        sender = lax.rem(node + nodes - hop, nodes)
        remote(
            bias_all.at[sender],
            bias_all.at[sender],
            b_s.at[hop - 1],
            b_r.at[hop - 1],
            (lax.rem(node + hop, nodes), feat),
        ).wait_recv()
    bias_total = bias_all[0]
    for part in range(1, nodes):
        bias_total = bias_total + bias_all[part]
    bgrad_ref[...] = bias_total

    for slot, copy in enumerate(z_copies):
        copy.wait()
        wgrad_ref[...] += z_recv[slot].astype(jnp.float32)
    for copy in started:
        copy.wait_send()


def layer(rows, flat_weight, out_bias, cotangent):
    nodes, feats = lax.axis_size("node"), lax.axis_size("feat")
    highs, depths = feats // 2, nodes // 2
    total_rows, width = rows.shape
    outs = flat_weight.shape[0]
    own_rows = cotangent.shape[0]
    units = outs // nodes
    cols = max(2 * units, 128)
    pieces = outs // cols
    fars = max(1, highs - 1)
    dma = pltpu.SemaphoreType.DMA
    vmem = pl.BlockSpec(memory_space=pltpu.VMEM)
    flops = 4 * total_rows * width * outs
    return pl.pallas_call(
        functools.partial(layer_kernel, nodes, feats, cols),
        out_shape=(
            jax.ShapeDtypeStruct((own_rows, outs), jnp.bfloat16),
            jax.ShapeDtypeStruct((units, width), jnp.float32),
            jax.ShapeDtypeStruct((1, outs), jnp.float32),
        ),
        in_specs=[vmem] * 4,
        out_specs=(vmem,) * 3,
        scratch_shapes=[
            pltpu.VMEM((pieces, total_rows, cols), jnp.float32),
            pltpu.VMEM((pieces, highs, own_rows, cols), jnp.float32),
            pltpu.VMEM((pieces, own_rows, cols), jnp.float32),
            pltpu.VMEM((pieces, fars, own_rows, cols), jnp.bfloat16),
            pltpu.VMEM((pieces, fars, own_rows, cols), jnp.bfloat16),
            pltpu.VMEM((pieces, total_rows, cols), jnp.bfloat16),
            pltpu.VMEM((cols, width), jnp.float32),
            pltpu.VMEM((depths, units, width), jnp.bfloat16),
            pltpu.VMEM((depths, units, width), jnp.bfloat16),
            pltpu.VMEM((depths, units, width), jnp.float32),
            pltpu.VMEM((depths, units, width), jnp.bfloat16),
            pltpu.VMEM((depths, units, width), jnp.bfloat16),
            pltpu.VMEM((nodes, 1, outs), jnp.float32),
            dma((pieces, highs)),
            dma((pieces, highs)),
            dma((pieces, fars)),
            dma((pieces, fars)),
            dma((pieces,)),
            dma((pieces,)),
            dma((pieces, fars)),
            dma((pieces, fars)),
            dma((pieces, fars)),
            dma((pieces, fars)),
            dma((depths,)),
            dma((depths,)),
            dma((depths,)),
            dma((depths,)),
            dma((nodes,)),
            dma((nodes,)),
        ],
        compiler_params=pltpu.CompilerParams(
            collective_id=0, has_side_effects=True, vmem_limit_bytes=48 * 1024 * 1024
        ),
        cost_estimate=pl.CostEstimate(
            flops=flops, bytes_accessed=8 * total_rows * outs, transcendentals=own_rows * outs
        ),
        name="layer",
    )(rows, flat_weight, out_bias[None, :], cotangent)


def local(
    features,
    degrees,
    tile_row,
    tile_col,
    tile_count,
    send_block,
    tile_val,
    weight,
    out_bias,
    cotangent,
):
    row_scale = lax.rsqrt(degrees.astype(jnp.float32))[:, None]
    flat_weight = lax.all_gather(weight.reshape(weight.shape[0], -1), "node", axis=0, tiled=True)
    matrix = dense_matrix(tile_row, tile_col, tile_count, tile_val, features.shape[0])
    rows = hops(features, row_scale, matrix, send_block, tile_val.shape[-1])
    output, weight_grad, bias_grad = layer(rows, flat_weight, out_bias, cotangent)
    return (output, weight_grad.reshape(weight.shape), bias_grad[0])


def solution(mesh):
    in_specs = (
        P("node", "feat"),
        P("node"),
        P("node", None),
        P("node", None),
        P("node"),
        P(),
        P("node", None, None, None),
        P("node", None, "feat"),
        P(),
        P(("node", "feat"), None),
    )
    out_specs = (P(("node", "feat"), None), P("node", None, "feat"), P())
    return jax.shard_map(local, mesh=mesh, in_specs=in_specs, out_specs=out_specs, check_vma=False)
```

```python
import functools

import jax
import jax.numpy as jnp
from jax import lax
from jax.experimental import pallas as pl
from jax.experimental.pallas import tpu as pltpu
from jax.sharding import PartitionSpec as P

HOPS = 2
MESH = pl.DeviceIdType.MESH


def matrix_kernel(tile_row, tile_col, tile_count, tile_val, matrix):
    block = tile_val.shape[-1]
    matrix[...] = jnp.zeros_like(matrix)

    def place(tile, carry):
        row = pl.multiple_of(tile_row[0, tile] * block, block)
        col = pl.multiple_of(tile_col[0, tile] * block, block)
        here = (pl.ds(row, block), pl.ds(col, block))
        total = matrix[here].astype(jnp.float32) + tile_val[0, tile].astype(jnp.float32)
        matrix[here] = total.astype(jnp.bfloat16)
        return carry

    lax.fori_loop(0, tile_count[0], place, 0)


def dense_matrix(tile_row, tile_col, tile_count, tile_val, own_nodes):
    block = tile_val.shape[-1]
    columns = own_nodes + lax.axis_size("node") * block
    smem = pl.BlockSpec(memory_space=pltpu.SMEM)
    vmem = pl.BlockSpec(memory_space=pltpu.VMEM)
    return pl.pallas_call(
        matrix_kernel,
        out_shape=jax.ShapeDtypeStruct((own_nodes, columns), jnp.bfloat16),
        in_specs=[smem, smem, smem, vmem],
        out_specs=vmem,
        compiler_params=pltpu.CompilerParams(vmem_limit_bytes=40 * 1024 * 1024),
        name="matrix",
    )(tile_row, tile_col, tile_count, tile_val)


def hops_kernel(
    nodes,
    send_block,
    features,
    scale,
    matrix,
    weight,
    rows,
    full,
    source,
    outgoing,
    frame,
    acc,
    s_sem,
    r_sem,
    z_s,
    z_r,
    x_s,
    x_r,
):
    node = lax.axis_index("node")
    feat = lax.axis_index("feat")
    own_nodes, panel = features.shape
    block = frame.shape[2]
    barrier = pltpu.get_barrier_semaphore()
    for hop in range(1, nodes):
        pl.semaphore_signal(
            barrier, inc=1, device_id=(lax.rem(node + hop, nodes), feat), device_id_type=MESH
        )

    def put_source(values):
        source[...] = values.astype(jnp.bfloat16).reshape(source.shape)

    put_source(features[...] * scale[...])
    rows[:, pl.ds(0, panel)] = features[...].astype(jnp.bfloat16)
    pl.semaphore_wait(barrier, nodes - 1)

    units = weight.shape[0]
    lane, depth = lax.rem(node, 2), node // 2
    depths = nodes // 2
    ways = ((0, 2), (1, -2))

    def unit_copy(origin, s, r, device):
        part = full.at[pl.ds(pl.multiple_of(origin * units, 16), units), :]
        return pltpu.make_async_remote_copy(
            src_ref=part,
            dst_ref=part,
            send_sem=s,
            recv_sem=r,
            device_id=device,
            device_id_type=MESH,
        )

    def reaches(way, turn):
        return depth >= turn if way == 0 else depth + turn < depths

    def goes_on(way):
        return depth + 1 < depths if way == 0 else depth > 0

    def along(way, shift, turn, start_turn):
        return unit_copy(
            node - shift * turn,
            z_s.at[way, start_turn],
            z_r.at[way, start_turn],
            (node + shift, feat),
        )

    def across(way, shift, turn, origin_lane):
        return unit_copy(
            (depth - (shift // 2) * turn) * 2 + origin_lane,
            x_s.at[way, turn],
            x_r.at[way, turn],
            (node + 1 - 2 * lane, feat),
        )

    def weight_turn(turn):
        for way, shift in ways:

            @pl.when(reaches(way, turn))
            def _():
                if turn > 0:
                    along(way, shift, turn, turn - 1).wait_recv()

                @pl.when(goes_on(way))
                def _():
                    along(way, shift, turn, turn).start()

                if turn > 0 or way == 0:
                    across(way, shift, turn, lane).start()

    def weight_end():
        for turn in range(depths):
            for way, shift in ways:

                @pl.when(reaches(way, turn))
                def _():
                    @pl.when(goes_on(way))
                    def _():
                        along(way, shift, turn, turn).wait_send()

                    if turn > 0 or way == 0:
                        across(way, shift, turn, 1 - lane).wait_recv()
                        across(way, shift, turn, lane).wait_send()

    full[pl.ds(pl.multiple_of(node * units, 16), units), :] = weight[...]

    group = min(nodes, 8)
    copies = []
    for step in range(HOPS):
        arrivals = []
        for hop in range(1, nodes):
            part = lax.rem(node + hop, nodes)
            outgoing[step, hop - 1] = source[send_block[node, part]]
            copy = pltpu.make_async_remote_copy(
                src_ref=outgoing.at[step, hop - 1],
                dst_ref=frame.at[step, node],
                send_sem=s_sem.at[step, hop - 1],
                recv_sem=r_sem.at[step, hop - 1],
                device_id=(part, feat),
                device_id_type=MESH,
            )
            copy.start()
            copies.append(copy)
            sender = lax.rem(node + nodes - hop, nodes)
            arrivals.append(
                pltpu.make_async_remote_copy(
                    src_ref=outgoing.at[step, hop - 1],
                    dst_ref=frame.at[step, sender],
                    send_sem=s_sem.at[step, hop - 1],
                    recv_sem=r_sem.at[step, hop - 1],
                    device_id=(part, feat),
                    device_id_type=MESH,
                )
            )
        if step < depths:
            weight_turn(step)
        frame[step, node] = jnp.zeros((block, panel), jnp.bfloat16)
        acc[...] = jnp.dot(
            matrix[:, pl.ds(0, own_nodes)],
            source[...].reshape(own_nodes, panel),
            preferred_element_type=jnp.float32,
        )
        for arrival in arrivals:
            arrival.wait_recv()

        def add(first):
            start = pl.multiple_of(own_nodes + first * block, block)
            acc[...] += jnp.dot(
                matrix[:, pl.ds(start, group * block)],
                frame[step, pl.ds(first, group)].reshape(group * block, panel),
                preferred_element_type=jnp.float32,
            )

        if nodes == group:
            add(0)
        else:

            def add_group(index, carry):
                add(index * group)
                return carry

            lax.fori_loop(0, nodes // group, add_group, 0)
        hop_value = acc[...] * scale[...]
        rows[:, pl.ds((step + 1) * panel, panel)] = hop_value.astype(jnp.bfloat16)
        if step + 1 < HOPS:
            put_source(hop_value * scale[...])
    for turn in range(HOPS, depths):
        weight_turn(turn)
    weight_end()
    for copy in copies:
        copy.wait_send()


def hops(features, scale, matrix, send_block, weight, block):
    nodes = lax.axis_size("node")
    own_nodes, panel = features.shape
    smem = pl.BlockSpec(memory_space=pltpu.SMEM)
    vmem = pl.BlockSpec(memory_space=pltpu.VMEM)
    dma = pltpu.SemaphoreType.DMA
    return pl.pallas_call(
        functools.partial(hops_kernel, nodes),
        out_shape=(
            jax.ShapeDtypeStruct((own_nodes, (HOPS + 1) * panel), jnp.bfloat16),
            jax.ShapeDtypeStruct((nodes * weight.shape[0], weight.shape[1]), jnp.bfloat16),
        ),
        in_specs=[smem, vmem, vmem, vmem, vmem],
        out_specs=(vmem, vmem),
        scratch_shapes=[
            pltpu.VMEM((own_nodes // block, block, panel), jnp.bfloat16),
            pltpu.VMEM((HOPS, nodes - 1, block, panel), jnp.bfloat16),
            pltpu.VMEM((HOPS, nodes, block, panel), jnp.bfloat16),
            pltpu.VMEM((own_nodes, panel), jnp.float32),
            dma((HOPS, nodes - 1)),
            dma((HOPS, nodes - 1)),
            dma((2, nodes // 2)),
            dma((2, nodes // 2)),
            dma((2, nodes // 2)),
            dma((2, nodes // 2)),
        ],
        compiler_params=pltpu.CompilerParams(
            collective_id=1, has_side_effects=True, vmem_limit_bytes=48 * 1024 * 1024
        ),
        cost_estimate=pl.CostEstimate(
            flops=HOPS * 2 * matrix.shape[0] * matrix.shape[1] * panel,
            bytes_accessed=100 * 1024 * 1024,
            transcendentals=0,
        ),
        name="hops",
    )(send_block, features, scale, matrix, weight)


def layer_kernel(
    nodes,
    feats,
    cols,
    rows_ref,
    weight_ref,
    bias_ref,
    cot_ref,
    out_ref,
    wgrad_ref,
    bgrad_ref,
    terms,
    pair_recv,
    held,
    far_send,
    far_recv,
    grad_all,
    block,
    x_send,
    x_recv,
    x_held,
    z_send,
    z_recv,
    bias_all,
    pair_s,
    pair_r,
    far_s,
    far_r,
    gpair_s,
    gpair_r,
    gfar_s,
    gfar_r,
    gfwd_s,
    gfwd_r,
    x_s,
    x_r,
    z_s,
    z_r,
    b_s,
    b_r,
):
    node = lax.axis_index("node")
    feat = lax.axis_index("feat")
    side, high = lax.rem(feat, 2), feat // 2
    highs = feats // 2
    lane, depth = lax.rem(node, 2), node // 2
    own_rows = cot_ref.shape[0]
    units = wgrad_ref.shape[0]
    pieces = weight_ref.shape[0] // cols
    share = cols // (2 * units)
    pair = (node, feat + 1 - 2 * side)
    x_pair = (node + 1 - 2 * lane, feat)

    def far_feat(step):
        return lax.rem(high + 1 + step, highs) * 2 + side

    def window(index):
        piece = lax.rem(depth // share + 1 + index, pieces)
        return pl.ds(pl.multiple_of(piece * cols, cols), cols)

    def target(index, sub):
        piece = lax.rem(depth // share + 1 + index, pieces)
        return piece * share + lax.rem(lax.rem(depth, share) + 1 + sub, share)

    def chunk(owner):
        return pl.ds(pl.multiple_of(owner * own_rows, 16), own_rows)

    def remote(src, dst, s, r, device):
        return pltpu.make_async_remote_copy(
            src_ref=src,
            dst_ref=dst,
            send_sem=s,
            recv_sem=r,
            device_id=device,
            device_id_type=MESH,
        )

    barrier = pltpu.get_barrier_semaphore()
    pl.semaphore_signal(barrier, inc=1, device_id=pair, device_id_type=MESH)
    for step in range(highs - 1):
        pl.semaphore_signal(
            barrier, inc=1, device_id=(node, far_feat(step)), device_id_type=MESH
        )
    for step in range(1, nodes):
        pl.semaphore_signal(
            barrier, inc=1, device_id=(lax.rem(node + step, nodes), feat), device_id_type=MESH
        )

    started = []
    pair_copies = {}
    far_copies = {}
    near_grads = {}
    far_grads = {}
    x_copies = {}
    z_copies = []

    def make_terms(index):
        terms[index] = lax.dot_general(
            rows_ref[...],
            weight_ref[window(index), :],
            (((1,), (1,)), ((), ())),
            preferred_element_type=jnp.float32,
        )
        if index == 0:
            pl.semaphore_wait(barrier, highs + nodes - 1)
        for top in range(highs):
            copy = remote(
                terms.at[index, chunk(top * 2 + 1 - side), :],
                pair_recv.at[index, top],
                pair_s.at[index, top],
                pair_r.at[index, top],
                pair,
            )
            copy.start()
            pair_copies[index, top] = copy

    def add_pair(index):
        for top in range(highs):
            pair_copies[index, top].wait()
        for step in range(highs - 1):
            owner = far_feat(step)
            total = terms[index, chunk(owner), :] + pair_recv[index, owner // 2]
            far_send[index, step] = total.astype(jnp.bfloat16)
            copy = remote(
                far_send.at[index, step],
                far_recv.at[index, step],
                far_s.at[index, step],
                far_r.at[index, step],
                (node, owner),
            )
            copy.start()
            far_copies[index, step] = copy
        held[index] = terms[index, chunk(feat), :] + pair_recv[index, high]

    def make_grad(index):
        linear = held[index]
        for step in range(highs - 1):
            far_copies[index, step].wait()
            linear = linear + far_recv[index, step].astype(jnp.float32)
        linear = linear + bias_ref[:, window(index)]
        gate = 1.0 / (1.0 + jnp.exp(-linear))
        out_ref[:, window(index)] = (linear * gate).astype(jnp.bfloat16)
        slope = gate * (1.0 + linear * (1.0 - gate))
        grad = cot_ref[:, window(index)].astype(jnp.float32) * slope
        grad_all[index, chunk(feat), :] = grad.astype(jnp.bfloat16)
        mine = grad_all.at[index, chunk(feat), :]
        for step in range(highs - 1):
            copy = remote(
                mine, mine, gfar_s.at[index, step], gfar_r.at[index, step], (node, far_feat(step))
            )
            copy.start()
            started.append(copy)
        copy = remote(mine, mine, gpair_s.at[index], gpair_r.at[index], pair)
        copy.start()
        started.append(copy)

    def forward_grad(index):
        for step in range(highs - 1):
            origin = lax.rem(high + highs - 1 - step, highs) * 2 + side
            theirs = grad_all.at[index, chunk(origin), :]
            remote(
                theirs, theirs, gfar_s.at[index, step], gfar_r.at[index, step], pair
            ).wait_recv()
            copy = remote(theirs, theirs, gfwd_s.at[index, step], gfwd_r.at[index, step], pair)
            copy.start()
            started.append(copy)

    def weight_terms(index):
        other = grad_all.at[index, chunk(feat + 1 - 2 * side), :]
        remote(other, other, gpair_s.at[index], gpair_r.at[index], pair).wait_recv()
        for step in range(highs - 1):
            origin = lax.rem(high + highs - 1 - step, highs) * 2 + 1 - side
            theirs = grad_all.at[index, chunk(origin), :]
            remote(
                theirs, theirs, gfwd_s.at[index, step], gfwd_r.at[index, step], pair
            ).wait_recv()
        block[...] = lax.dot_general(
            grad_all[index],
            rows_ref[...],
            (((0,), (0,)), ((), ())),
            preferred_element_type=jnp.float32,
        )
        for sub in range(share):
            slot = index * share + sub
            start = lax.rem(lax.rem(depth, share) + 1 + sub, share) * (2 * units)
            theirs = pl.ds(pl.multiple_of(start + (1 - lane) * units, 16), units)
            mine = pl.ds(pl.multiple_of(start + lane * units, 16), units)
            x_send[slot] = block[theirs, :].astype(jnp.bfloat16)
            copy = remote(x_send.at[slot], x_recv.at[slot], x_s.at[slot], x_r.at[slot], x_pair)
            copy.start()
            x_copies[slot] = copy
            x_held[slot] = block[mine, :]
        bias_all[node, :, window(index)] = jnp.sum(
            grad_all[index].astype(jnp.float32), axis=0, keepdims=True
        )
        if index == pieces - 1:
            for hop in range(1, nodes):
                copy = remote(
                    bias_all.at[node],
                    bias_all.at[node],
                    b_s.at[hop - 1],
                    b_r.at[hop - 1],
                    (lax.rem(node + hop, nodes), feat),
                )
                copy.start()
                started.append(copy)

    def add_x(index):
        for sub in range(share):
            slot = index * share + sub
            x_copies[slot].wait()
            total = x_held[slot] + x_recv[slot].astype(jnp.float32)
            if slot == pieces * share - 1:
                wgrad_ref[...] = total
                continue
            z_send[slot] = total.astype(jnp.bfloat16)
            copy = remote(
                z_send.at[slot],
                z_recv.at[slot],
                z_s.at[slot],
                z_r.at[slot],
                (target(index, sub) * 2 + lane, feat),
            )
            copy.start()
            z_copies.append(copy)

    stages = (make_terms, add_pair, make_grad, forward_grad, weight_terms, add_x)
    for tick in range(pieces + len(stages) - 1):
        for order, stage in enumerate(stages):
            if 0 <= tick - order < pieces:
                stage(tick - order)

    for hop in range(1, nodes):
        sender = lax.rem(node + nodes - hop, nodes)
        remote(
            bias_all.at[sender],
            bias_all.at[sender],
            b_s.at[hop - 1],
            b_r.at[hop - 1],
            (lax.rem(node + hop, nodes), feat),
        ).wait_recv()
    bias_total = bias_all[0]
    for part in range(1, nodes):
        bias_total = bias_total + bias_all[part]
    bgrad_ref[...] = bias_total

    for slot, copy in enumerate(z_copies):
        copy.wait()
        wgrad_ref[...] += z_recv[slot].astype(jnp.float32)
    for copy in started:
        copy.wait_send()


def layer(rows, flat_weight, out_bias, cotangent):
    nodes, feats = lax.axis_size("node"), lax.axis_size("feat")
    highs, depths = feats // 2, nodes // 2
    total_rows, width = rows.shape
    outs = flat_weight.shape[0]
    own_rows = cotangent.shape[0]
    units = outs // nodes
    cols = max(2 * units, 128)
    pieces = outs // cols
    fars = max(1, highs - 1)
    dma = pltpu.SemaphoreType.DMA
    vmem = pl.BlockSpec(memory_space=pltpu.VMEM)
    flops = 4 * total_rows * width * outs
    return pl.pallas_call(
        functools.partial(layer_kernel, nodes, feats, cols),
        out_shape=(
            jax.ShapeDtypeStruct((own_rows, outs), jnp.bfloat16),
            jax.ShapeDtypeStruct((units, width), jnp.float32),
            jax.ShapeDtypeStruct((1, outs), jnp.float32),
        ),
        in_specs=[vmem] * 4,
        out_specs=(vmem,) * 3,
        scratch_shapes=[
            pltpu.VMEM((pieces, total_rows, cols), jnp.float32),
            pltpu.VMEM((pieces, highs, own_rows, cols), jnp.float32),
            pltpu.VMEM((pieces, own_rows, cols), jnp.float32),
            pltpu.VMEM((pieces, fars, own_rows, cols), jnp.bfloat16),
            pltpu.VMEM((pieces, fars, own_rows, cols), jnp.bfloat16),
            pltpu.VMEM((pieces, total_rows, cols), jnp.bfloat16),
            pltpu.VMEM((cols, width), jnp.float32),
            pltpu.VMEM((depths, units, width), jnp.bfloat16),
            pltpu.VMEM((depths, units, width), jnp.bfloat16),
            pltpu.VMEM((depths, units, width), jnp.float32),
            pltpu.VMEM((depths, units, width), jnp.bfloat16),
            pltpu.VMEM((depths, units, width), jnp.bfloat16),
            pltpu.VMEM((nodes, 1, outs), jnp.float32),
            dma((pieces, highs)),
            dma((pieces, highs)),
            dma((pieces, fars)),
            dma((pieces, fars)),
            dma((pieces,)),
            dma((pieces,)),
            dma((pieces, fars)),
            dma((pieces, fars)),
            dma((pieces, fars)),
            dma((pieces, fars)),
            dma((depths,)),
            dma((depths,)),
            dma((depths,)),
            dma((depths,)),
            dma((nodes,)),
            dma((nodes,)),
        ],
        compiler_params=pltpu.CompilerParams(
            collective_id=0, has_side_effects=True, vmem_limit_bytes=48 * 1024 * 1024
        ),
        cost_estimate=pl.CostEstimate(
            flops=flops, bytes_accessed=8 * total_rows * outs, transcendentals=own_rows * outs
        ),
        name="layer",
    )(rows, flat_weight, out_bias[None, :], cotangent)


def local(
    features,
    degrees,
    tile_row,
    tile_col,
    tile_count,
    send_block,
    tile_val,
    weight,
    out_bias,
    cotangent,
):
    row_scale = lax.rsqrt(degrees.astype(jnp.float32))[:, None]
    own_weight = weight.reshape(weight.shape[0], -1)
    matrix = dense_matrix(tile_row, tile_col, tile_count, tile_val, features.shape[0])
    rows, flat_weight = hops(
        features, row_scale, matrix, send_block, own_weight, tile_val.shape[-1]
    )
    output, weight_grad, bias_grad = layer(rows, flat_weight, out_bias, cotangent)
    return (output, weight_grad.reshape(weight.shape), bias_grad[0])


def solution(mesh):
    in_specs = (
        P("node", "feat"),
        P("node"),
        P("node", None),
        P("node", None),
        P("node"),
        P(),
        P("node", None, None, None),
        P("node", None, "feat"),
        P(),
        P(("node", "feat"), None),
    )
    out_specs = (P(("node", "feat"), None), P("node", None, "feat"), P())
    return jax.shard_map(local, mesh=mesh, in_specs=in_specs, out_specs=out_specs, check_vma=False)
```

```python
import functools

import jax
import jax.numpy as jnp
from jax import lax
from jax.experimental import pallas as pl
from jax.experimental.pallas import tpu as pltpu
from jax.sharding import PartitionSpec as P

HOPS = 2
MESH = pl.DeviceIdType.MESH


def matrix_kernel(tile_row, tile_col, tile_count, tile_val, matrix):
    block = tile_val.shape[-1]
    matrix[...] = jnp.zeros_like(matrix)

    def place(tile, carry):
        row = pl.multiple_of(tile_row[0, tile] * block, block)
        col = pl.multiple_of(tile_col[0, tile] * block, block)
        here = (pl.ds(row, block), pl.ds(col, block))
        total = matrix[here].astype(jnp.float32) + tile_val[0, tile].astype(jnp.float32)
        matrix[here] = total.astype(jnp.bfloat16)
        return carry

    lax.fori_loop(0, tile_count[0], place, 0)


def dense_matrix(tile_row, tile_col, tile_count, tile_val, own_nodes):
    block = tile_val.shape[-1]
    columns = own_nodes + lax.axis_size("node") * block
    smem = pl.BlockSpec(memory_space=pltpu.SMEM)
    vmem = pl.BlockSpec(memory_space=pltpu.VMEM)
    return pl.pallas_call(
        matrix_kernel,
        out_shape=jax.ShapeDtypeStruct((own_nodes, columns), jnp.bfloat16),
        in_specs=[smem, smem, smem, vmem],
        out_specs=vmem,
        compiler_params=pltpu.CompilerParams(vmem_limit_bytes=40 * 1024 * 1024),
        name="matrix",
    )(tile_row, tile_col, tile_count, tile_val)


def hops_kernel(
    nodes,
    send_block,
    features,
    scale,
    matrix,
    weight,
    rows,
    full,
    source,
    outgoing,
    frame,
    acc,
    s_sem,
    r_sem,
    z_s,
    z_r,
    x_s,
    x_r,
):
    node = lax.axis_index("node")
    feat = lax.axis_index("feat")
    own_nodes, panel = features.shape
    block = frame.shape[2]
    barrier = pltpu.get_barrier_semaphore()
    for hop in range(1, nodes):
        pl.semaphore_signal(
            barrier, inc=1, device_id=(lax.rem(node + hop, nodes), feat), device_id_type=MESH
        )

    def put_source(values):
        source[...] = values.astype(jnp.bfloat16).reshape(source.shape)

    put_source(features[...] * scale[...])
    rows[:, pl.ds(0, panel)] = features[...].astype(jnp.bfloat16)
    pl.semaphore_wait(barrier, nodes - 1)

    units = weight.shape[1]
    lane, depth = lax.rem(node, 2), node // 2
    depths = nodes // 2
    ways = ((0, 2), (1, -2))

    def unit_copy(origin, s, r, device):
        part = full.at[pl.ds(pl.multiple_of(origin * units, 16), units), :]
        return pltpu.make_async_remote_copy(
            src_ref=part,
            dst_ref=part,
            send_sem=s,
            recv_sem=r,
            device_id=device,
            device_id_type=MESH,
        )

    def reaches(way, turn):
        return depth >= turn if way == 0 else depth + turn < depths

    def goes_on(way):
        return depth + 1 < depths if way == 0 else depth > 0

    def along(way, shift, turn, start_turn):
        return unit_copy(
            node - shift * turn,
            z_s.at[way, start_turn],
            z_r.at[way, start_turn],
            (node + shift, feat),
        )

    def across(way, shift, turn, origin_lane):
        return unit_copy(
            (depth - (shift // 2) * turn) * 2 + origin_lane,
            x_s.at[way, turn],
            x_r.at[way, turn],
            (node + 1 - 2 * lane, feat),
        )

    def weight_turn(turn):
        for way, shift in ways:

            @pl.when(reaches(way, turn))
            def _():
                if turn > 0:
                    along(way, shift, turn, turn - 1).wait_recv()

                @pl.when(goes_on(way))
                def _():
                    along(way, shift, turn, turn).start()

                if turn > 0 or way == 0:
                    across(way, shift, turn, lane).start()

    def weight_end():
        for turn in range(depths):
            for way, shift in ways:

                @pl.when(reaches(way, turn))
                def _():
                    @pl.when(goes_on(way))
                    def _():
                        along(way, shift, turn, turn).wait_send()

                    if turn > 0 or way == 0:
                        across(way, shift, turn, 1 - lane).wait_recv()
                        across(way, shift, turn, lane).wait_send()

    for kind in range(weight.shape[0]):
        full[
            pl.ds(pl.multiple_of(node * units, 16), units), pl.ds(kind * panel, panel)
        ] = weight[kind]

    group = min(nodes, 8)
    copies = []
    for step in range(HOPS):
        arrivals = []
        for hop in range(1, nodes):
            part = lax.rem(node + hop, nodes)
            outgoing[step, hop - 1] = source[send_block[node, part]]
            copy = pltpu.make_async_remote_copy(
                src_ref=outgoing.at[step, hop - 1],
                dst_ref=frame.at[step, node],
                send_sem=s_sem.at[step, hop - 1],
                recv_sem=r_sem.at[step, hop - 1],
                device_id=(part, feat),
                device_id_type=MESH,
            )
            copy.start()
            copies.append(copy)
            sender = lax.rem(node + nodes - hop, nodes)
            arrivals.append(
                pltpu.make_async_remote_copy(
                    src_ref=outgoing.at[step, hop - 1],
                    dst_ref=frame.at[step, sender],
                    send_sem=s_sem.at[step, hop - 1],
                    recv_sem=r_sem.at[step, hop - 1],
                    device_id=(part, feat),
                    device_id_type=MESH,
                )
            )
        if step < depths:
            weight_turn(step)
        frame[step, node] = jnp.zeros((block, panel), jnp.bfloat16)
        acc[...] = jnp.dot(
            matrix[:, pl.ds(0, own_nodes)],
            source[...].reshape(own_nodes, panel),
            preferred_element_type=jnp.float32,
        )
        if step == HOPS - 1 and HOPS < depths:
            weight_turn(HOPS)
        for arrival in arrivals:
            arrival.wait_recv()

        def add(first):
            start = pl.multiple_of(own_nodes + first * block, block)
            acc[...] += jnp.dot(
                matrix[:, pl.ds(start, group * block)],
                frame[step, pl.ds(first, group)].reshape(group * block, panel),
                preferred_element_type=jnp.float32,
            )

        if nodes == group:
            add(0)
        else:

            def add_group(index, carry):
                add(index * group)
                return carry

            lax.fori_loop(0, nodes // group, add_group, 0)
        hop_value = acc[...] * scale[...]
        rows[:, pl.ds((step + 1) * panel, panel)] = hop_value.astype(jnp.bfloat16)
        if step + 1 < HOPS:
            put_source(hop_value * scale[...])
    for turn in range(HOPS + 1, depths):
        weight_turn(turn)
    weight_end()
    for copy in copies:
        copy.wait_send()


def hops(features, scale, matrix, send_block, weight, block):
    nodes = lax.axis_size("node")
    own_nodes, panel = features.shape
    smem = pl.BlockSpec(memory_space=pltpu.SMEM)
    vmem = pl.BlockSpec(memory_space=pltpu.VMEM)
    dma = pltpu.SemaphoreType.DMA
    return pl.pallas_call(
        functools.partial(hops_kernel, nodes),
        out_shape=(
            jax.ShapeDtypeStruct((own_nodes, (HOPS + 1) * panel), jnp.bfloat16),
            jax.ShapeDtypeStruct((nodes * weight.shape[1], (HOPS + 1) * panel), jnp.bfloat16),
        ),
        in_specs=[smem, vmem, vmem, vmem, vmem],
        out_specs=(vmem, vmem),
        scratch_shapes=[
            pltpu.VMEM((own_nodes // block, block, panel), jnp.bfloat16),
            pltpu.VMEM((HOPS, nodes - 1, block, panel), jnp.bfloat16),
            pltpu.VMEM((HOPS, nodes, block, panel), jnp.bfloat16),
            pltpu.VMEM((own_nodes, panel), jnp.float32),
            dma((HOPS, nodes - 1)),
            dma((HOPS, nodes - 1)),
            dma((2, nodes // 2)),
            dma((2, nodes // 2)),
            dma((2, nodes // 2)),
            dma((2, nodes // 2)),
        ],
        compiler_params=pltpu.CompilerParams(
            collective_id=1, has_side_effects=True, vmem_limit_bytes=48 * 1024 * 1024
        ),
        cost_estimate=pl.CostEstimate(
            flops=HOPS * 2 * matrix.shape[0] * matrix.shape[1] * panel,
            bytes_accessed=100 * 1024 * 1024,
            transcendentals=0,
        ),
        name="hops",
    )(send_block, features, scale, matrix, weight)


def layer_kernel(
    nodes,
    feats,
    cols,
    rows_ref,
    weight_ref,
    bias_ref,
    cot_ref,
    out_ref,
    wgrad_ref,
    bgrad_ref,
    terms,
    pair_recv,
    held,
    far_send,
    far_recv,
    grad_all,
    block,
    x_send,
    x_recv,
    x_held,
    z_send,
    z_recv,
    bias_all,
    pair_s,
    pair_r,
    far_s,
    far_r,
    gpair_s,
    gpair_r,
    gfar_s,
    gfar_r,
    gfwd_s,
    gfwd_r,
    x_s,
    x_r,
    z_s,
    z_r,
    b_s,
    b_r,
):
    node = lax.axis_index("node")
    feat = lax.axis_index("feat")
    side, high = lax.rem(feat, 2), feat // 2
    highs = feats // 2
    lane, depth = lax.rem(node, 2), node // 2
    own_rows = cot_ref.shape[0]
    units = wgrad_ref.shape[1]
    pieces = weight_ref.shape[0] // cols
    share = cols // (2 * units)
    pair = (node, feat + 1 - 2 * side)
    x_pair = (node + 1 - 2 * lane, feat)

    def far_feat(step):
        return lax.rem(high + 1 + step, highs) * 2 + side

    def window(index):
        piece = lax.rem(depth // share + 1 + index, pieces)
        return pl.ds(pl.multiple_of(piece * cols, cols), cols)

    def target(index, sub):
        piece = lax.rem(depth // share + 1 + index, pieces)
        return piece * share + lax.rem(lax.rem(depth, share) + 1 + sub, share)

    def chunk(owner):
        return pl.ds(pl.multiple_of(owner * own_rows, 16), own_rows)

    def remote(src, dst, s, r, device):
        return pltpu.make_async_remote_copy(
            src_ref=src,
            dst_ref=dst,
            send_sem=s,
            recv_sem=r,
            device_id=device,
            device_id_type=MESH,
        )

    barrier = pltpu.get_barrier_semaphore()
    pl.semaphore_signal(barrier, inc=1, device_id=pair, device_id_type=MESH)
    for step in range(highs - 1):
        pl.semaphore_signal(
            barrier, inc=1, device_id=(node, far_feat(step)), device_id_type=MESH
        )
    for step in range(1, nodes):
        pl.semaphore_signal(
            barrier, inc=1, device_id=(lax.rem(node + step, nodes), feat), device_id_type=MESH
        )

    started = []
    pair_copies = {}
    far_copies = {}
    near_grads = {}
    far_grads = {}
    x_copies = {}
    z_copies = []

    def make_terms(index):
        terms[index] = lax.dot_general(
            rows_ref[...],
            weight_ref[window(index), :],
            (((1,), (1,)), ((), ())),
            preferred_element_type=jnp.float32,
        )
        if index == 0:
            pl.semaphore_wait(barrier, highs + nodes - 1)
        for top in range(highs):
            copy = remote(
                terms.at[index, chunk(top * 2 + 1 - side), :],
                pair_recv.at[index, top],
                pair_s.at[index, top],
                pair_r.at[index, top],
                pair,
            )
            copy.start()
            pair_copies[index, top] = copy

    def add_pair(index):
        for top in range(highs):
            pair_copies[index, top].wait()
        for step in range(highs - 1):
            owner = far_feat(step)
            total = terms[index, chunk(owner), :] + pair_recv[index, owner // 2]
            far_send[index, step] = total.astype(jnp.bfloat16)
            copy = remote(
                far_send.at[index, step],
                far_recv.at[index, step],
                far_s.at[index, step],
                far_r.at[index, step],
                (node, owner),
            )
            copy.start()
            far_copies[index, step] = copy
        held[index] = terms[index, chunk(feat), :] + pair_recv[index, high]

    def make_grad(index):
        linear = held[index]
        for step in range(highs - 1):
            far_copies[index, step].wait()
            linear = linear + far_recv[index, step].astype(jnp.float32)
        linear = linear + bias_ref[:, window(index)]
        gate = 1.0 / (1.0 + jnp.exp(-linear))
        out_ref[:, window(index)] = (linear * gate).astype(jnp.bfloat16)
        slope = gate * (1.0 + linear * (1.0 - gate))
        grad = cot_ref[:, window(index)].astype(jnp.float32) * slope
        grad_all[index, chunk(feat), :] = grad.astype(jnp.bfloat16)
        mine = grad_all.at[index, chunk(feat), :]
        for step in range(highs - 1):
            copy = remote(
                mine, mine, gfar_s.at[index, step], gfar_r.at[index, step], (node, far_feat(step))
            )
            copy.start()
            started.append(copy)
        copy = remote(mine, mine, gpair_s.at[index], gpair_r.at[index], pair)
        copy.start()
        started.append(copy)

    def forward_grad(index):
        for step in range(highs - 1):
            origin = lax.rem(high + highs - 1 - step, highs) * 2 + side
            theirs = grad_all.at[index, chunk(origin), :]
            remote(
                theirs, theirs, gfar_s.at[index, step], gfar_r.at[index, step], pair
            ).wait_recv()
            copy = remote(theirs, theirs, gfwd_s.at[index, step], gfwd_r.at[index, step], pair)
            copy.start()
            started.append(copy)

    def weight_terms(index):
        other = grad_all.at[index, chunk(feat + 1 - 2 * side), :]
        remote(other, other, gpair_s.at[index], gpair_r.at[index], pair).wait_recv()
        for step in range(highs - 1):
            origin = lax.rem(high + highs - 1 - step, highs) * 2 + 1 - side
            theirs = grad_all.at[index, chunk(origin), :]
            remote(
                theirs, theirs, gfwd_s.at[index, step], gfwd_r.at[index, step], pair
            ).wait_recv()
        block[...] = lax.dot_general(
            grad_all[index],
            rows_ref[...],
            (((0,), (0,)), ((), ())),
            preferred_element_type=jnp.float32,
        )
        for sub in range(share):
            slot = index * share + sub
            start = lax.rem(lax.rem(depth, share) + 1 + sub, share) * (2 * units)
            theirs = pl.ds(pl.multiple_of(start + (1 - lane) * units, 16), units)
            mine = pl.ds(pl.multiple_of(start + lane * units, 16), units)
            x_send[slot] = block[theirs, :].astype(jnp.bfloat16)
            copy = remote(x_send.at[slot], x_recv.at[slot], x_s.at[slot], x_r.at[slot], x_pair)
            copy.start()
            x_copies[slot] = copy
            x_held[slot] = block[mine, :]
        bias_all[node, :, window(index)] = jnp.sum(
            grad_all[index].astype(jnp.float32), axis=0, keepdims=True
        )
        if index == pieces - 1:
            for hop in range(1, nodes):
                copy = remote(
                    bias_all.at[node],
                    bias_all.at[node],
                    b_s.at[hop - 1],
                    b_r.at[hop - 1],
                    (lax.rem(node + hop, nodes), feat),
                )
                copy.start()
                started.append(copy)

    def add_x(index):
        for sub in range(share):
            slot = index * share + sub
            x_copies[slot].wait()
            total = x_held[slot] + x_recv[slot].astype(jnp.float32)
            if slot == pieces * share - 1:
                x_held[slot] = total
                continue
            z_send[slot] = total.astype(jnp.bfloat16)
            copy = remote(
                z_send.at[slot],
                z_recv.at[slot],
                z_s.at[slot],
                z_r.at[slot],
                (target(index, sub) * 2 + lane, feat),
            )
            copy.start()
            z_copies.append(copy)

    stages = (make_terms, add_pair, make_grad, forward_grad, weight_terms, add_x)
    for tick in range(pieces + len(stages) - 1):
        for order, stage in enumerate(stages):
            if 0 <= tick - order < pieces:
                stage(tick - order)

    for hop in range(1, nodes):
        sender = lax.rem(node + nodes - hop, nodes)
        remote(
            bias_all.at[sender],
            bias_all.at[sender],
            b_s.at[hop - 1],
            b_r.at[hop - 1],
            (lax.rem(node + hop, nodes), feat),
        ).wait_recv()
    bias_total = bias_all[0]
    for part in range(1, nodes):
        bias_total = bias_total + bias_all[part]
    bgrad_ref[...] = bias_total

    last = pieces * share - 1
    for slot, copy in enumerate(z_copies):
        copy.wait()
        x_held[last] += z_recv[slot].astype(jnp.float32)
    panel = wgrad_ref.shape[2]
    for kind in range(wgrad_ref.shape[0]):
        wgrad_ref[kind] = x_held[last, :, pl.ds(kind * panel, panel)]
    for copy in started:
        copy.wait_send()


def layer(rows, flat_weight, out_bias, cotangent):
    nodes, feats = lax.axis_size("node"), lax.axis_size("feat")
    highs, depths = feats // 2, nodes // 2
    total_rows, width = rows.shape
    outs = flat_weight.shape[0]
    own_rows = cotangent.shape[0]
    units = outs // nodes
    cols = max(2 * units, 128)
    pieces = outs // cols
    fars = max(1, highs - 1)
    dma = pltpu.SemaphoreType.DMA
    vmem = pl.BlockSpec(memory_space=pltpu.VMEM)
    flops = 4 * total_rows * width * outs
    return pl.pallas_call(
        functools.partial(layer_kernel, nodes, feats, cols),
        out_shape=(
            jax.ShapeDtypeStruct((own_rows, outs), jnp.bfloat16),
            jax.ShapeDtypeStruct((HOPS + 1, units, width // (HOPS + 1)), jnp.float32),
            jax.ShapeDtypeStruct((1, outs), jnp.float32),
        ),
        in_specs=[vmem] * 4,
        out_specs=(vmem,) * 3,
        scratch_shapes=[
            pltpu.VMEM((pieces, total_rows, cols), jnp.float32),
            pltpu.VMEM((pieces, highs, own_rows, cols), jnp.float32),
            pltpu.VMEM((pieces, own_rows, cols), jnp.float32),
            pltpu.VMEM((pieces, fars, own_rows, cols), jnp.bfloat16),
            pltpu.VMEM((pieces, fars, own_rows, cols), jnp.bfloat16),
            pltpu.VMEM((pieces, total_rows, cols), jnp.bfloat16),
            pltpu.VMEM((cols, width), jnp.float32),
            pltpu.VMEM((depths, units, width), jnp.bfloat16),
            pltpu.VMEM((depths, units, width), jnp.bfloat16),
            pltpu.VMEM((depths, units, width), jnp.float32),
            pltpu.VMEM((depths, units, width), jnp.bfloat16),
            pltpu.VMEM((depths, units, width), jnp.bfloat16),
            pltpu.VMEM((nodes, 1, outs), jnp.float32),
            dma((pieces, highs)),
            dma((pieces, highs)),
            dma((pieces, fars)),
            dma((pieces, fars)),
            dma((pieces,)),
            dma((pieces,)),
            dma((pieces, fars)),
            dma((pieces, fars)),
            dma((pieces, fars)),
            dma((pieces, fars)),
            dma((depths,)),
            dma((depths,)),
            dma((depths,)),
            dma((depths,)),
            dma((nodes,)),
            dma((nodes,)),
        ],
        compiler_params=pltpu.CompilerParams(
            collective_id=0, has_side_effects=True, vmem_limit_bytes=48 * 1024 * 1024
        ),
        cost_estimate=pl.CostEstimate(
            flops=flops, bytes_accessed=8 * total_rows * outs, transcendentals=own_rows * outs
        ),
        name="layer",
    )(rows, flat_weight, out_bias[None, :], cotangent)


def local(
    features,
    degrees,
    tile_row,
    tile_col,
    tile_count,
    send_block,
    tile_val,
    weight,
    out_bias,
    cotangent,
):
    row_scale = lax.rsqrt(degrees.astype(jnp.float32))[:, None]
    own_weight = weight.transpose(1, 0, 2)
    matrix = dense_matrix(tile_row, tile_col, tile_count, tile_val, features.shape[0])
    rows, flat_weight = hops(
        features, row_scale, matrix, send_block, own_weight, tile_val.shape[-1]
    )
    output, weight_grad, bias_grad = layer(rows, flat_weight, out_bias, cotangent)
    return (output, weight_grad.transpose(1, 0, 2), bias_grad[0])


def solution(mesh):
    in_specs = (
        P("node", "feat"),
        P("node"),
        P("node", None),
        P("node", None),
        P("node"),
        P(),
        P("node", None, None, None),
        P("node", None, "feat"),
        P(),
        P(("node", "feat"), None),
    )
    out_specs = (P(("node", "feat"), None), P("node", None, "feat"), P())
    return jax.shard_map(local, mesh=mesh, in_specs=in_specs, out_specs=out_specs, check_vma=False)
```

```python
import functools

import jax
import jax.numpy as jnp
from jax import lax
from jax.experimental import pallas as pl
from jax.experimental.pallas import tpu as pltpu
from jax.sharding import PartitionSpec as P

HOPS = 2
MESH = pl.DeviceIdType.MESH


def matrix_kernel(tile_row, tile_col, tile_count, tile_val, matrix):
    block = tile_val.shape[-1]
    matrix[...] = jnp.zeros_like(matrix)

    def place(tile, carry):
        row = pl.multiple_of(tile_row[0, tile] * block, block)
        col = pl.multiple_of(tile_col[0, tile] * block, block)
        here = (pl.ds(row, block), pl.ds(col, block))
        total = matrix[here].astype(jnp.float32) + tile_val[0, tile].astype(jnp.float32)
        matrix[here] = total.astype(jnp.bfloat16)
        return carry

    lax.fori_loop(0, tile_count[0], place, 0)


def dense_matrix(tile_row, tile_col, tile_count, tile_val, own_nodes):
    block = tile_val.shape[-1]
    columns = own_nodes + lax.axis_size("node") * block
    smem = pl.BlockSpec(memory_space=pltpu.SMEM)
    vmem = pl.BlockSpec(memory_space=pltpu.VMEM)
    return pl.pallas_call(
        matrix_kernel,
        out_shape=jax.ShapeDtypeStruct((own_nodes, columns), jnp.bfloat16),
        in_specs=[smem, smem, smem, vmem],
        out_specs=vmem,
        compiler_params=pltpu.CompilerParams(vmem_limit_bytes=40 * 1024 * 1024),
        name="matrix",
    )(tile_row, tile_col, tile_count, tile_val)


def hops_kernel(
    nodes,
    send_block,
    features,
    scale,
    matrix,
    weight,
    rows,
    full,
    source,
    outgoing,
    frame,
    acc,
    s_sem,
    r_sem,
    z_s,
    z_r,
    x_s,
    x_r,
):
    node = lax.axis_index("node")
    feat = lax.axis_index("feat")
    own_nodes, panel = features.shape
    block = frame.shape[2]
    barrier = pltpu.get_barrier_semaphore()
    for hop in range(1, nodes):
        pl.semaphore_signal(
            barrier, inc=1, device_id=(lax.rem(node + hop, nodes), feat), device_id_type=MESH
        )

    def put_source(values):
        source[...] = values.astype(jnp.bfloat16).reshape(source.shape)

    put_source(features[...] * scale[...])
    rows[:, pl.ds(0, panel)] = features[...].astype(jnp.bfloat16)
    pl.semaphore_wait(barrier, nodes - 1)

    units = weight.shape[1]
    lane, depth = lax.rem(node, 2), node // 2
    depths = nodes // 2
    ways = ((0, 2), (1, -2))

    def unit_copy(origin, s, r, device):
        part = full.at[pl.ds(pl.multiple_of(origin * units, 16), units), :]
        return pltpu.make_async_remote_copy(
            src_ref=part,
            dst_ref=part,
            send_sem=s,
            recv_sem=r,
            device_id=device,
            device_id_type=MESH,
        )

    def reaches(way, turn):
        return depth >= turn if way == 0 else depth + turn < depths

    def goes_on(way):
        return depth + 1 < depths if way == 0 else depth > 0

    def along(way, shift, turn, start_turn):
        return unit_copy(
            node - shift * turn,
            z_s.at[way, start_turn],
            z_r.at[way, start_turn],
            (node + shift, feat),
        )

    def across(way, shift, turn, origin_lane):
        return unit_copy(
            (depth - (shift // 2) * turn) * 2 + origin_lane,
            x_s.at[way, turn],
            x_r.at[way, turn],
            (node + 1 - 2 * lane, feat),
        )

    def weight_turn(turn):
        for way, shift in ways:

            @pl.when(reaches(way, turn))
            def _():
                if turn > 0:
                    along(way, shift, turn, turn - 1).wait_recv()

                @pl.when(goes_on(way))
                def _():
                    along(way, shift, turn, turn).start()

                if turn > 0 or way == 0:
                    across(way, shift, turn, lane).start()

    def weight_end():
        for turn in range(depths):
            for way, shift in ways:

                @pl.when(reaches(way, turn))
                def _():
                    @pl.when(goes_on(way))
                    def _():
                        along(way, shift, turn, turn).wait_send()

                    if turn > 0 or way == 0:
                        across(way, shift, turn, 1 - lane).wait_recv()
                        across(way, shift, turn, lane).wait_send()

    for kind in range(weight.shape[0]):
        full[
            pl.ds(pl.multiple_of(node * units, 16), units), pl.ds(kind * panel, panel)
        ] = weight[kind]

    group = min(nodes, 8)
    copies = []
    for step in range(HOPS):
        arrivals = []
        for hop in range(1, nodes):
            part = lax.rem(node + hop, nodes)
            outgoing[step, hop - 1] = source[send_block[node, part]]
            copy = pltpu.make_async_remote_copy(
                src_ref=outgoing.at[step, hop - 1],
                dst_ref=frame.at[step, node],
                send_sem=s_sem.at[step, hop - 1],
                recv_sem=r_sem.at[step, hop - 1],
                device_id=(part, feat),
                device_id_type=MESH,
            )
            copy.start()
            copies.append(copy)
            sender = lax.rem(node + nodes - hop, nodes)
            arrivals.append(
                pltpu.make_async_remote_copy(
                    src_ref=outgoing.at[step, hop - 1],
                    dst_ref=frame.at[step, sender],
                    send_sem=s_sem.at[step, hop - 1],
                    recv_sem=r_sem.at[step, hop - 1],
                    device_id=(part, feat),
                    device_id_type=MESH,
                )
            )
        if 2 * step < depths:
            weight_turn(2 * step)
        frame[step, node] = jnp.zeros((block, panel), jnp.bfloat16)
        acc[...] = jnp.dot(
            matrix[:, pl.ds(0, own_nodes)],
            source[...].reshape(own_nodes, panel),
            preferred_element_type=jnp.float32,
        )
        if 2 * step + 1 < depths:
            weight_turn(2 * step + 1)
        for arrival in arrivals:
            arrival.wait_recv()

        def add(first):
            start = pl.multiple_of(own_nodes + first * block, block)
            acc[...] += jnp.dot(
                matrix[:, pl.ds(start, group * block)],
                frame[step, pl.ds(first, group)].reshape(group * block, panel),
                preferred_element_type=jnp.float32,
            )

        if nodes == group:
            add(0)
        else:

            def add_group(index, carry):
                add(index * group)
                return carry

            lax.fori_loop(0, nodes // group, add_group, 0)
        hop_value = acc[...] * scale[...]
        rows[:, pl.ds((step + 1) * panel, panel)] = hop_value.astype(jnp.bfloat16)
        if step + 1 < HOPS:
            put_source(hop_value * scale[...])
    for turn in range(2 * HOPS, depths):
        weight_turn(turn)
    weight_end()
    for copy in copies:
        copy.wait_send()


def hops(features, scale, matrix, send_block, weight, block):
    nodes = lax.axis_size("node")
    own_nodes, panel = features.shape
    smem = pl.BlockSpec(memory_space=pltpu.SMEM)
    vmem = pl.BlockSpec(memory_space=pltpu.VMEM)
    dma = pltpu.SemaphoreType.DMA
    return pl.pallas_call(
        functools.partial(hops_kernel, nodes),
        out_shape=(
            jax.ShapeDtypeStruct((own_nodes, (HOPS + 1) * panel), jnp.bfloat16),
            jax.ShapeDtypeStruct((nodes * weight.shape[1], (HOPS + 1) * panel), jnp.bfloat16),
        ),
        in_specs=[smem, vmem, vmem, vmem, vmem],
        out_specs=(vmem, vmem),
        scratch_shapes=[
            pltpu.VMEM((own_nodes // block, block, panel), jnp.bfloat16),
            pltpu.VMEM((HOPS, nodes - 1, block, panel), jnp.bfloat16),
            pltpu.VMEM((HOPS, nodes, block, panel), jnp.bfloat16),
            pltpu.VMEM((own_nodes, panel), jnp.float32),
            dma((HOPS, nodes - 1)),
            dma((HOPS, nodes - 1)),
            dma((2, nodes // 2)),
            dma((2, nodes // 2)),
            dma((2, nodes // 2)),
            dma((2, nodes // 2)),
        ],
        compiler_params=pltpu.CompilerParams(
            collective_id=1, has_side_effects=True, vmem_limit_bytes=48 * 1024 * 1024
        ),
        cost_estimate=pl.CostEstimate(
            flops=HOPS * 2 * matrix.shape[0] * matrix.shape[1] * panel,
            bytes_accessed=100 * 1024 * 1024,
            transcendentals=0,
        ),
        name="hops",
    )(send_block, features, scale, matrix, weight)


def layer_kernel(
    nodes,
    feats,
    cols,
    rows_ref,
    weight_ref,
    bias_ref,
    cot_ref,
    out_ref,
    wgrad_ref,
    bgrad_ref,
    terms,
    pair_recv,
    held,
    far_send,
    far_recv,
    grad_all,
    block,
    x_send,
    x_recv,
    x_held,
    z_send,
    z_recv,
    bias_all,
    pair_s,
    pair_r,
    far_s,
    far_r,
    gpair_s,
    gpair_r,
    gfar_s,
    gfar_r,
    gfwd_s,
    gfwd_r,
    x_s,
    x_r,
    z_s,
    z_r,
    b_s,
    b_r,
):
    node = lax.axis_index("node")
    feat = lax.axis_index("feat")
    side, high = lax.rem(feat, 2), feat // 2
    highs = feats // 2
    lane, depth = lax.rem(node, 2), node // 2
    own_rows = cot_ref.shape[0]
    units = wgrad_ref.shape[1]
    pieces = weight_ref.shape[0] // cols
    share = cols // (2 * units)
    pair = (node, feat + 1 - 2 * side)
    x_pair = (node + 1 - 2 * lane, feat)

    def far_feat(step):
        return lax.rem(high + 1 + step, highs) * 2 + side

    def window(index):
        piece = lax.rem(depth // share + 1 + index, pieces)
        return pl.ds(pl.multiple_of(piece * cols, cols), cols)

    def target(index, sub):
        piece = lax.rem(depth // share + 1 + index, pieces)
        return piece * share + lax.rem(lax.rem(depth, share) + 1 + sub, share)

    def chunk(owner):
        return pl.ds(pl.multiple_of(owner * own_rows, 16), own_rows)

    def remote(src, dst, s, r, device):
        return pltpu.make_async_remote_copy(
            src_ref=src,
            dst_ref=dst,
            send_sem=s,
            recv_sem=r,
            device_id=device,
            device_id_type=MESH,
        )

    barrier = pltpu.get_barrier_semaphore()
    pl.semaphore_signal(barrier, inc=1, device_id=pair, device_id_type=MESH)
    for step in range(highs - 1):
        pl.semaphore_signal(
            barrier, inc=1, device_id=(node, far_feat(step)), device_id_type=MESH
        )
    for step in range(1, nodes):
        pl.semaphore_signal(
            barrier, inc=1, device_id=(lax.rem(node + step, nodes), feat), device_id_type=MESH
        )

    started = []
    pair_copies = {}
    far_copies = {}
    near_grads = {}
    far_grads = {}
    x_copies = {}
    z_copies = []

    def make_terms(index):
        terms[index] = lax.dot_general(
            rows_ref[...],
            weight_ref[window(index), :],
            (((1,), (1,)), ((), ())),
            preferred_element_type=jnp.float32,
        )
        if index == 0:
            pl.semaphore_wait(barrier, highs + nodes - 1)
        for top in range(highs):
            copy = remote(
                terms.at[index, chunk(top * 2 + 1 - side), :],
                pair_recv.at[index, top],
                pair_s.at[index, top],
                pair_r.at[index, top],
                pair,
            )
            copy.start()
            pair_copies[index, top] = copy

    def add_pair(index):
        for top in range(highs):
            pair_copies[index, top].wait()
        for step in range(highs - 1):
            owner = far_feat(step)
            total = terms[index, chunk(owner), :] + pair_recv[index, owner // 2]
            far_send[index, step] = total.astype(jnp.bfloat16)
            copy = remote(
                far_send.at[index, step],
                far_recv.at[index, step],
                far_s.at[index, step],
                far_r.at[index, step],
                (node, owner),
            )
            copy.start()
            far_copies[index, step] = copy
        held[index] = terms[index, chunk(feat), :] + pair_recv[index, high]

    def make_grad(index):
        linear = held[index]
        for step in range(highs - 1):
            far_copies[index, step].wait()
            linear = linear + far_recv[index, step].astype(jnp.float32)
        linear = linear + bias_ref[:, window(index)]
        gate = 1.0 / (1.0 + jnp.exp(-linear))
        out_ref[:, window(index)] = (linear * gate).astype(jnp.bfloat16)
        slope = gate * (1.0 + linear * (1.0 - gate))
        grad = cot_ref[:, window(index)].astype(jnp.float32) * slope
        grad_all[index, chunk(feat), :] = grad.astype(jnp.bfloat16)
        mine = grad_all.at[index, chunk(feat), :]
        for step in range(highs - 1):
            copy = remote(
                mine, mine, gfar_s.at[index, step], gfar_r.at[index, step], (node, far_feat(step))
            )
            copy.start()
            started.append(copy)
        copy = remote(mine, mine, gpair_s.at[index], gpair_r.at[index], pair)
        copy.start()
        started.append(copy)

    def forward_grad(index):
        for step in range(highs - 1):
            origin = lax.rem(high + highs - 1 - step, highs) * 2 + side
            theirs = grad_all.at[index, chunk(origin), :]
            remote(
                theirs, theirs, gfar_s.at[index, step], gfar_r.at[index, step], pair
            ).wait_recv()
            copy = remote(theirs, theirs, gfwd_s.at[index, step], gfwd_r.at[index, step], pair)
            copy.start()
            started.append(copy)

    def weight_terms(index):
        other = grad_all.at[index, chunk(feat + 1 - 2 * side), :]
        remote(other, other, gpair_s.at[index], gpair_r.at[index], pair).wait_recv()
        for step in range(highs - 1):
            origin = lax.rem(high + highs - 1 - step, highs) * 2 + 1 - side
            theirs = grad_all.at[index, chunk(origin), :]
            remote(
                theirs, theirs, gfwd_s.at[index, step], gfwd_r.at[index, step], pair
            ).wait_recv()
        block[...] = lax.dot_general(
            grad_all[index],
            rows_ref[...],
            (((0,), (0,)), ((), ())),
            preferred_element_type=jnp.float32,
        )
        for sub in range(share):
            slot = index * share + sub
            start = lax.rem(lax.rem(depth, share) + 1 + sub, share) * (2 * units)
            theirs = pl.ds(pl.multiple_of(start + (1 - lane) * units, 16), units)
            mine = pl.ds(pl.multiple_of(start + lane * units, 16), units)
            x_send[slot] = block[theirs, :].astype(jnp.bfloat16)
            copy = remote(x_send.at[slot], x_recv.at[slot], x_s.at[slot], x_r.at[slot], x_pair)
            copy.start()
            x_copies[slot] = copy
            x_held[slot] = block[mine, :]
        bias_all[node, :, window(index)] = jnp.sum(
            grad_all[index].astype(jnp.float32), axis=0, keepdims=True
        )
        if index == pieces - 1:
            for hop in range(1, nodes):
                copy = remote(
                    bias_all.at[node],
                    bias_all.at[node],
                    b_s.at[hop - 1],
                    b_r.at[hop - 1],
                    (lax.rem(node + hop, nodes), feat),
                )
                copy.start()
                started.append(copy)

    def add_x(index):
        for sub in range(share):
            slot = index * share + sub
            x_copies[slot].wait()
            total = x_held[slot] + x_recv[slot].astype(jnp.float32)
            if slot == pieces * share - 1:
                x_held[slot] = total
                continue
            z_send[slot] = total.astype(jnp.bfloat16)
            copy = remote(
                z_send.at[slot],
                z_recv.at[slot],
                z_s.at[slot],
                z_r.at[slot],
                (target(index, sub) * 2 + lane, feat),
            )
            copy.start()
            z_copies.append(copy)

    stages = (make_terms, add_pair, make_grad, forward_grad, weight_terms, add_x)
    for tick in range(pieces + len(stages) - 1):
        for order, stage in enumerate(stages):
            if 0 <= tick - order < pieces:
                stage(tick - order)

    for hop in range(1, nodes):
        sender = lax.rem(node + nodes - hop, nodes)
        remote(
            bias_all.at[sender],
            bias_all.at[sender],
            b_s.at[hop - 1],
            b_r.at[hop - 1],
            (lax.rem(node + hop, nodes), feat),
        ).wait_recv()
    bias_total = bias_all[0]
    for part in range(1, nodes):
        bias_total = bias_total + bias_all[part]
    bgrad_ref[...] = bias_total

    last = pieces * share - 1
    for slot, copy in enumerate(z_copies):
        copy.wait()
        x_held[last] += z_recv[slot].astype(jnp.float32)
    panel = wgrad_ref.shape[2]
    for kind in range(wgrad_ref.shape[0]):
        wgrad_ref[kind] = x_held[last, :, pl.ds(kind * panel, panel)]
    for copy in started:
        copy.wait_send()


def layer(rows, flat_weight, out_bias, cotangent):
    nodes, feats = lax.axis_size("node"), lax.axis_size("feat")
    highs, depths = feats // 2, nodes // 2
    total_rows, width = rows.shape
    outs = flat_weight.shape[0]
    own_rows = cotangent.shape[0]
    units = outs // nodes
    cols = max(2 * units, 128)
    pieces = outs // cols
    fars = max(1, highs - 1)
    dma = pltpu.SemaphoreType.DMA
    vmem = pl.BlockSpec(memory_space=pltpu.VMEM)
    flops = 4 * total_rows * width * outs
    return pl.pallas_call(
        functools.partial(layer_kernel, nodes, feats, cols),
        out_shape=(
            jax.ShapeDtypeStruct((own_rows, outs), jnp.bfloat16),
            jax.ShapeDtypeStruct((HOPS + 1, units, width // (HOPS + 1)), jnp.float32),
            jax.ShapeDtypeStruct((1, outs), jnp.float32),
        ),
        in_specs=[vmem] * 4,
        out_specs=(vmem,) * 3,
        scratch_shapes=[
            pltpu.VMEM((pieces, total_rows, cols), jnp.float32),
            pltpu.VMEM((pieces, highs, own_rows, cols), jnp.float32),
            pltpu.VMEM((pieces, own_rows, cols), jnp.float32),
            pltpu.VMEM((pieces, fars, own_rows, cols), jnp.bfloat16),
            pltpu.VMEM((pieces, fars, own_rows, cols), jnp.bfloat16),
            pltpu.VMEM((pieces, total_rows, cols), jnp.bfloat16),
            pltpu.VMEM((cols, width), jnp.float32),
            pltpu.VMEM((depths, units, width), jnp.bfloat16),
            pltpu.VMEM((depths, units, width), jnp.bfloat16),
            pltpu.VMEM((depths, units, width), jnp.float32),
            pltpu.VMEM((depths, units, width), jnp.bfloat16),
            pltpu.VMEM((depths, units, width), jnp.bfloat16),
            pltpu.VMEM((nodes, 1, outs), jnp.float32),
            dma((pieces, highs)),
            dma((pieces, highs)),
            dma((pieces, fars)),
            dma((pieces, fars)),
            dma((pieces,)),
            dma((pieces,)),
            dma((pieces, fars)),
            dma((pieces, fars)),
            dma((pieces, fars)),
            dma((pieces, fars)),
            dma((depths,)),
            dma((depths,)),
            dma((depths,)),
            dma((depths,)),
            dma((nodes,)),
            dma((nodes,)),
        ],
        compiler_params=pltpu.CompilerParams(
            collective_id=0, has_side_effects=True, vmem_limit_bytes=48 * 1024 * 1024
        ),
        cost_estimate=pl.CostEstimate(
            flops=flops, bytes_accessed=8 * total_rows * outs, transcendentals=own_rows * outs
        ),
        name="layer",
    )(rows, flat_weight, out_bias[None, :], cotangent)


def local(
    features,
    degrees,
    tile_row,
    tile_col,
    tile_count,
    send_block,
    tile_val,
    weight,
    out_bias,
    cotangent,
):
    row_scale = lax.rsqrt(degrees.astype(jnp.float32))[:, None]
    own_weight = weight.transpose(1, 0, 2)
    matrix = dense_matrix(tile_row, tile_col, tile_count, tile_val, features.shape[0])
    rows, flat_weight = hops(
        features, row_scale, matrix, send_block, own_weight, tile_val.shape[-1]
    )
    output, weight_grad, bias_grad = layer(rows, flat_weight, out_bias, cotangent)
    return (output, weight_grad.transpose(1, 0, 2), bias_grad[0])


def solution(mesh):
    in_specs = (
        P("node", "feat"),
        P("node"),
        P("node", None),
        P("node", None),
        P("node"),
        P(),
        P("node", None, None, None),
        P("node", None, "feat"),
        P(),
        P(("node", "feat"), None),
    )
    out_specs = (P(("node", "feat"), None), P("node", None, "feat"), P())
    return jax.shard_map(local, mesh=mesh, in_specs=in_specs, out_specs=out_specs, check_vma=False)
```
